256 devices in a mesh: pre: 2 (over x_lo), dec: 64 (over z, y, core), rep: 2 (over x_hi).
Axes of the slice: x: 4 (x_hi: 2, x_lo: 2; x = x_hi * 2 + x_lo), y: 4, z: 8, core: 2. Of those that a mesh axis runs over, the one named last changes fastest.
Arguments:
- queries: bfloat16 [4096, 128, 576], P('dec', ('pre', 'rep')), may hold values from -170 to 170
- prefix_of: int32 [4096, 1], P('dec'), may hold values from 0 to 63; in each aligned block of 64 rows (0 to 63, 64 to 127, ...) at most 2 rows name the same one
- prefix_cache: bfloat16 [64, 1024, 576], P('dec'), may hold values from -6 to 6
- suffix_cache: bfloat16 [4096, 32, 576], P('dec'), may hold values from -6 to 6
- suffix_len: int32 [4096], P('dec'), may hold values from 1 to 32
- fresh_pages: bfloat16 [4096, 64, 576], P('dec', ('pre', 'rep')), may hold values from -6 to 6
- page_owner: int32 [4096, 1], replicated, may hold values from 0 to 63; in each aligned block of 64 rows (0 to 63, 64 to 127, ...) at most 2 rows name the same one
- page_request: int32 [4096], replicated, may hold values from 0 to 63
- page_tokens: int32 [4096], replicated, may hold values from 1 to 64
- value_up: bfloat16 [128, 512, 128], P(('pre', 'rep')), may hold values from -0.25 to 0.25
Outputs:
- attn_out: bfloat16 [4096, 16384], P('dec', ('pre', 'rep'))
The draws below stay inside these ranges and needn't reach their ends.
Inputs may be any that keep to these rules, and one draw needn't show every extreme that they name: `prefix_of`: among the 64 requests of one index of dec (aligned blocks of rows), no prefix is named more than 2 times. `page_owner`: among the 64 fresh pages of one index of dec (aligned blocks of rows), no owner is named more than 2 times.
All inputs are finite; a program needn't handle non-finite values.
Results may differ from the reference program's by a relative error of at most 0.011.
Values may be sent and summed in bfloat16 or wider, within the bound.
A program may use at most 256 MiB of HBM per device.

```python
import math
import jax
import jax.numpy as jnp
import numpy as np
from jax import lax

H = 128
DL = 512
DV = 128
DQ = 576
PAGE = 64
PLEN = 1024
SUF = 32
R_DEV = 64
PFX = 64
REQ = 4096
NEWP = 4096
CAP = 2
N_DEC = 64


def draw_queries(key, part):
    key = jax.random.fold_in(key, 11)
    base_key, scale_key = jax.random.split(key, 2)
    row_scale = jnp.exp(jax.random.uniform(scale_key, (REQ, H, 1), jnp.float32, math.log(0.25), math.log(2.5)))
    base = jax.random.truncated_normal(base_key, -4.0, 4.0, (REQ, H, DQ), jnp.float32)
    return (base * row_scale).astype(jnp.bfloat16)


def plant(entries, own_key, low, largest):
    place = [jax.random.randint(jax.random.fold_in(own_key, axis), (), 0, length) for axis, length in enumerate(entries.shape)]
    longest = entries.shape.index(max(entries.shape))
    neighbour = place[:longest] + [(place[longest] + 1) % entries.shape[longest]] + place[longest + 1:]
    return entries.at[tuple(place)].set(low).at[tuple(neighbour)].set(largest)


def levels(rng, shape, cuts, smallest, top_value):
    gain = 1.0
    for position, parts in cuts:
        heights = jax.random.uniform(jax.random.fold_in(jax.random.fold_in(rng, 6), position), (parts,), jnp.float32, smallest / len(cuts), top_value / len(cuts))
        gain = gain * jnp.repeat(jnp.exp(heights), shape[position] // parts).reshape((-1,) + (1,) * (len(shape) - 1 - position))
    return gain


def shared_out(rng, own, number, rows, number_of, top, bound, slope):
    ranking = jax.random.permutation(rng, number_of)
    packed, ordinary = portions_of(number_of, rows * top, bound, slope, True), portions_of(number_of, rows * top, bound, slope, False)
    places = jnp.arange(number_of)

    def named(lengths, offset_by):
        used = int((lengths > 0).sum())
        fixed = max(1, used // 4)
        moved = fixed + (places - fixed + offset_by * (used - fixed)) % max(1, number_of - fixed)
        return jnp.zeros((number_of,), jnp.int32).at[ranking[jnp.where(places < fixed, places, moved)]].set(jnp.asarray(lengths, jnp.int32))

    lengths = jnp.where(number % 4 == 0, named(packed, number // 4), named(ordinary, number - number // 4 - 1))
    mixed = jax.random.permutation(jax.random.fold_in(own, 3), number_of)
    giver, taker = mixed[0:number_of // 2 * 2:2], mixed[1:number_of // 2 * 2:2]
    slack = jnp.minimum(lengths[giver] - 1, bound - lengths[taker]) // 2
    slack = jnp.where((giver == ranking[0]) | (taker == ranking[0]) | (lengths[taker] == 0), 0, jnp.maximum(slack, 0))
    moved = jax.random.randint(jax.random.fold_in(own, 4), (number_of // 2,), 0, 1 << 20) % (slack + 1)
    lengths = lengths.at[giver].add(-moved).at[taker].add(moved)
    members = jnp.searchsorted(jnp.cumsum(lengths), jnp.arange(rows * top), side="right").astype(jnp.int32)
    table = members.reshape(top, rows).T
    table = table[jax.random.permutation(jax.random.fold_in(own, 1), rows)]
    offset_by = jax.random.randint(jax.random.fold_in(own, 2), (rows, 1), 0, top)
    return jnp.take_along_axis(table, (jnp.arange(top)[None, :] + offset_by) % top, axis=1)


def portions_of(amount, total, limit, slope, full):
    weights = [(1 << 20) // math.isqrt(grade ** slope) + 1 for grade in range(1, amount + 1)]
    largest = limit if full else min(limit, max(-(-total // amount), total * weights[0] // sum(weights)))
    least = 1 if total - largest >= amount - 1 else 0
    given, spare = [largest] + [least] * (amount - 1), total - largest - least * (amount - 1)
    while spare > 0:
        candidates = [i for i in range(1, amount) if given[i] < largest] or [i for i in range(1, amount) if given[i] < limit]
        pool, left = sum([weights[i] for i in candidates]), spare
        for i in candidates:
            addition = min(limit - given[i], max(1, left * weights[i] // pool), spare)
            given[i] = given[i] + addition
            spare = spare - addition
    return np.array(given)


def normal_values(rng, extent, deviation, bound, cuts=(), held_as=jnp.bfloat16):
    loudness = levels(rng, extent, cuts, -0.22, 0.18) if cuts else 1.0
    drawn = jax.random.normal(rng, extent, jnp.float32) * deviation * loudness
    return jnp.minimum(jnp.maximum(drawn, -bound), bound).astype(held_as)


def setup_inputs(seed: int = 0) -> dict:
    key_list = jax.random.split(jax.random.key(seed), 11)
    queries = draw_queries(jax.random.fold_in(key_list[10], 71), 0)
    prefix_of_keys = jax.random.split(jax.random.fold_in(key_list[1], 1), REQ // R_DEV)
    prefix_of_turns = jax.random.permutation(jax.random.fold_in(key_list[1], 3), REQ // R_DEV)
    prefix_of = jax.vmap(lambda own, number: shared_out(jax.random.fold_in(key_list[1], 2), own, number, R_DEV, PFX, 1, CAP, 2))(prefix_of_keys, prefix_of_turns).reshape((REQ, 1))
    prefix_cache = normal_values(key_list[2], (PFX, PLEN, DQ), 1.0, 6.0, ((0, 64),))
    suffix_cache = normal_values(key_list[3], (REQ, SUF, DQ), 1.0, 6.0, ((0, 64),))
    suffix_len = plant(jax.random.randint(key_list[4], (REQ,), 1, SUF + 1), jax.random.fold_in(key_list[4], 1), 1, SUF).astype(jnp.int32)
    fresh_pages = normal_values(key_list[5], (NEWP, PAGE, DQ), 1.0, 6.0, ((0, 64), (1, 4)))
    page_owner_keys = jax.random.split(jax.random.fold_in(key_list[6], 1), NEWP // R_DEV)
    page_owner_turns = jax.random.permutation(jax.random.fold_in(key_list[6], 3), NEWP // R_DEV)
    page_owner = jax.vmap(lambda own, number: shared_out(jax.random.fold_in(key_list[6], 2), own, number, R_DEV, N_DEC, 1, CAP, 2))(page_owner_keys, page_owner_turns).reshape((NEWP, 1))
    page_request = plant(jax.random.randint(key_list[7], (NEWP,), 0, R_DEV), jax.random.fold_in(key_list[7], 1), 0, R_DEV - 1).astype(jnp.int32)
    page_tokens = plant(jax.random.randint(key_list[8], (NEWP,), 1, PAGE + 1), jax.random.fold_in(key_list[8], 1), 1, PAGE).astype(jnp.int32)
    value_up = normal_values(key_list[9], (H, DL, DV), DL ** -0.5, 0.25, ((0, 4),))
    return {"queries": queries, "prefix_of": prefix_of, "prefix_cache": prefix_cache, "suffix_cache": suffix_cache, "suffix_len": suffix_len, "fresh_pages": fresh_pages, "page_owner": page_owner, "page_request": page_request, "page_tokens": page_tokens, "value_up": value_up}


softmax_scale = 192.0 ** -0.5
neg_fill = -1.0e30


def block_partial(queried, key_rows, allowed):
    scores = jnp.einsum("brd,btd->brt", queried, key_rows, precision=lax.Precision.HIGHEST) * softmax_scale
    scores = jnp.where(allowed, scores, neg_fill)
    maxima = jnp.max(scores, axis=-1)
    weights = jnp.exp(scores - maxima[..., None]).astype(jnp.bfloat16)
    weights = lax.optimization_barrier(weights).astype(jnp.float32)
    totals = jnp.sum(weights, axis=-1)
    summed = jnp.einsum("brt,btd->brd", weights, key_rows[..., :DL], precision=lax.Precision.HIGHEST)
    return summed, maxima, totals


def reference(queries, prefix_of, prefix_cache, suffix_cache, suffix_len, fresh_pages, page_owner, page_request, page_tokens, value_up):
    owners_all = page_owner[:, 0]
    page_index = jnp.arange(NEWP, dtype=jnp.int32)
    value_wide = value_up.astype(jnp.float32)

    def owner_out(owner):
        first_row = (owner * R_DEV).astype(jnp.int32)
        queried = lax.dynamic_slice_in_dim(queries, first_row, R_DEV, 0).astype(jnp.float32)
        chosen_prefix = lax.dynamic_slice_in_dim(prefix_of, first_row, R_DEV, 0)[:, 0]
        prefix_keys = prefix_cache[chosen_prefix].astype(jnp.float32)
        prefix_sum, prefix_max, prefix_total = block_partial(queried, prefix_keys, True)
        resident_keys = lax.dynamic_slice_in_dim(suffix_cache, first_row, R_DEV, 0).astype(jnp.float32)
        resident_lengths = lax.dynamic_slice_in_dim(suffix_len, first_row, R_DEV, 0)
        resident_ok = jnp.arange(SUF, dtype=jnp.int32)[None, None, :] < resident_lengths[:, None, None]
        resident_sum, resident_max, resident_total = block_partial(queried, resident_keys, resident_ok)
        order_key = jnp.where(owners_all == owner, 0, 1).astype(jnp.int32) * NEWP + page_index
        picked = jnp.argsort(order_key)[: N_DEC * CAP].astype(jnp.int32)
        alive = owners_all[picked] == owner
        page_req = page_request[picked]
        page_len = jnp.where(alive, page_tokens[picked], 0)
        page_ok = jnp.arange(PAGE, dtype=jnp.int32)[None, None, :] < page_len[:, None, None]
        page_keys = fresh_pages[picked].astype(jnp.float32)
        page_sum, page_max, page_total = block_partial(queried[page_req], page_keys, page_ok)
        member = (page_req[:, None] == jnp.arange(R_DEV, dtype=jnp.int32)[None, :]) & alive[:, None]
        fresh_best = jnp.max(jnp.where(member[:, :, None], page_max[:, None, :], neg_fill), axis=0)
        highest = jnp.maximum(jnp.maximum(prefix_max, resident_max), fresh_best)
        prefix_coef = jnp.exp(prefix_max - highest)
        resident_coef = jnp.exp(resident_max - highest)
        page_coef = jnp.exp(page_max - highest[page_req]) * alive[:, None].astype(jnp.float32)
        member_f = member.astype(jnp.float32)
        denominator = prefix_coef * prefix_total + resident_coef * resident_total + jnp.einsum("sr,sh->rh", member_f, page_coef * page_total, precision=lax.Precision.HIGHEST)
        numerator = prefix_coef[..., None] * prefix_sum + resident_coef[..., None] * resident_sum + jnp.einsum("sr,shd->rhd", member_f, page_coef[..., None] * page_sum, precision=lax.Precision.HIGHEST)
        latent_out = numerator / denominator[..., None]
        mixed = jnp.einsum("rhd,hde->rhe", latent_out, value_wide, precision=lax.Precision.HIGHEST)
        return mixed.astype(jnp.bfloat16).reshape(R_DEV, H * DV)

    blocks = lax.map(owner_out, jnp.arange(N_DEC, dtype=jnp.int32))
    return blocks.reshape(REQ, H * DV)
```

```python
import functools

import jax
import jax.numpy as jnp
from jax import lax
from jax.experimental import pallas as pl
from jax.experimental.pallas import tpu as pltpu
from jax.sharding import PartitionSpec as P

MESH = pl.DeviceIdType.MESH
BF, F32 = jnp.bfloat16, jnp.float32
ANY = pl.BlockSpec(memory_space=pl.ANY)
VM = pl.BlockSpec(memory_space=pltpu.VMEM)
SM = pl.BlockSpec(memory_space=pltpu.SMEM)
DL, DQ = 512, 576
SCALE = 192.0**-0.5
NEG = -1e30
ORDER = (0, 1, -1, 2, -2, 3, -3, 4)
D, Q = 512, 128
PIECE = 128
DQDS = (((1, 0)), ((-1, 0)), ((1, 1)), ((-1, 1)), ((2, 0)), ((2, 1)), ((0, 1)))


def bucket_kernel(pref, owner, queries, fresh, qs, ps, slot, count):
    dec = lax.axis_index("dec")
    qs[...] = jnp.zeros_like(qs)
    ps[...] = jnp.zeros_like(ps)

    def clear(i, c):
        count[0, i] = 0
        count[1, i] = 0
        return c

    lax.fori_loop(0, 64, clear, 0, unroll=8)

    def put(i, c):
        p = pref[i]
        k = count[0, p]
        count[0, p] = k + 1
        to = (p % 8) * 16 + (p // 8) * 2 + k
        qs[to] = queries[i]
        slot[i] = to
        o = owner[dec * 64 + i]
        k = count[1, o]
        count[1, o] = k + 1
        ps[o * 2 + k] = fresh[i]
        return c

    lax.fori_loop(0, 64, put, 0)


def bucket(pref, owner, queries, fresh):
    qs, ps, slot = pl.pallas_call(
        bucket_kernel,
        out_shape=(
            jax.ShapeDtypeStruct((128, 32, DQ), BF),
            jax.ShapeDtypeStruct((128, 16, DQ), BF),
            jax.ShapeDtypeStruct((64,), jnp.int32),
        ),
        in_specs=[SM, SM, VM, VM],
        out_specs=(VM, VM, SM),
        scratch_shapes=[pltpu.SMEM((2, 64), jnp.int32)],
        compiler_params=pltpu.CompilerParams(vmem_limit_bytes=40 * 2**20),
    )(pref, owner, queries, fresh)
    return qs.reshape(8, 8, 2, 32, DQ), ps.reshape(64, 2, 16, DQ), slot


def rcopy(src, dst, ss, rs, dev):
    return pltpu.make_async_remote_copy(
        src_ref=src, dst_ref=dst, send_sem=ss, recv_sem=rs, device_id=dev, device_id_type=MESH
    )


def nt(a, b):
    return lax.dot_general(a, b, (((1,), (1,)), ((), ())), preferred_element_type=F32)


def nn(a, b):
    return jnp.dot(a, b, preferred_element_type=F32)


def exchange_kernel(
    qs, pf, ps, vu, W, ret, rlse,
    qr, pa, lat, lse, outs, lses,
    qss, qrs, rss, rrs, pss, prs, xss, xrs, yss, yrs, bss, brs, loc,
):
    pre, dec, rep = lax.axis_index("pre"), lax.axis_index("dec"), lax.axis_index("rep")
    z, y, core = dec // 8, (dec // 2) % 4, dec % 2
    yc = dec % 8
    x = rep * 2 + pre
    g = pre * 2 + rep

    def at_x(v):
        v = v % 4
        return (v % 2, dec, v // 2)

    def g_of(v):
        v = v % 4
        return (v % 2) * 2 + v // 2

    right, left = at_x(x + 1), at_x(x + 3)
    bar = pltpu.get_barrier_semaphore()

    def hello(o, c):
        pl.semaphore_signal(bar, inc=1, device_id=(pre, (dec + o) % 64, rep), device_id_type=MESH)
        return c

    lax.fori_loop(1, 64, hello, 0)
    pl.semaphore_signal(bar, inc=1, device_id=right, device_id_type=MESH)
    pl.semaphore_signal(bar, inc=1, device_id=left, device_id_type=MESH)
    pl.semaphore_wait(bar, 65)

    def start(c):
        c.start()
        return c

    own_q = start(pltpu.make_async_copy(qs.at[yc], qr.at[:, yc], loc.at[0]))
    own_p = start(pltpu.make_async_copy(pf, pa.at[z], loc.at[1]))
    own_w = start(pltpu.make_async_copy(ps.at[dec], W.at[dec, :, g], loc.at[2]))

    def peer(dy, dc):
        return ((y + dy + 4) % 4) * 2 + (core + dc) % 2

    def query_send(j, n):
        dy, dc = DQDS[n]
        t = peer(dy, dc)
        part = pl.ds(2 * j, 2)
        return start(rcopy(qs.at[t, part], qr.at[part, yc], qss.at[n], qrs.at[n], (pre, z * 8 + t, rep)))

    def query_wait(n):
        dy, dc = DQDS[n]
        s = peer(-dy, dc)
        return rcopy(qs.at[0], qr.at[:, s], qss.at[n], qrs.at[n], (pre, z * 8 + s, rep))

    def zdev(dz):
        return (pre, ((z + dz + 8) % 8) * 8 + yc, rep)

    def piece(n, last, dirn):
        if n == 0:
            return pl.ds(D + g * Q + dirn * (Q // 2), Q // 2) if last else pl.ds(D + g * Q, Q)
        return pl.ds((n - 1) * PIECE, PIECE)

    def pieces(dirn, t):
        if t < 4:
            return (0, 1, 2, 3, 4)
        return (0, 1, 2) if dirn == 0 else (0, 3, 4)

    rings = {}

    def ring_start(dirn, t, n):
        sgn = 1 - 2 * dirn
        blk = (z - sgn * (t - 1) + 8) % 8
        rows = piece(n, t == 4, dirn)
        src = pf.at[rows] if t == 1 else pa.at[blk, rows]
        rings[dirn, t, n] = start(
            rcopy(src, pa.at[blk, rows], rss.at[dirn, t - 1, n], rrs.at[dirn, t - 1, n], zdev(sgn))
        )

    def page_send(b):
        dz = ORDER[b]

        def one(o, c):
            t = ((z + dz + 8) % 8) * 8 + (yc + o) % 8
            rcopy(ps.at[t], W.at[dec, :, g], pss.at[b], prs.at[b], (pre, t, rep)).start()
            return c

        lax.fori_loop(1 if dz == 0 else 0, 8, one, 0)

    def batch(b):
        return pl.ds(((z - ORDER[b] + 8) % 8) * 8, 8)

    def page_wait(b):
        w = W.at[pl.ds(0, 7 if ORDER[b] == 0 else 8), :, 0]
        c = rcopy(w, w, pss.at[b], prs.at[b], right)
        c.wait_send()
        c.wait_recv()

    xs = {}

    def x_start(b):
        r = W.at[batch(b), :, g]
        xs[b] = [
            start(rcopy(r, r, xss.at[0, b], xrs.at[0, b], right)),
            start(rcopy(r, r, xss.at[1, b], xrs.at[1, b], left)),
        ]

    def x_forward(b):
        xs[b][0].wait_recv()
        r = W.at[batch(b), 0, g_of(x + 3)]
        xs[b].append(start(rcopy(r, r, xss.at[2, b], xrs.at[2, b], right)))
        xs[b][1].wait_recv()
        r = W.at[batch(b), 1, g_of(x + 1)]
        xs[b].append(start(rcopy(r, r, xss.at[3, b], xrs.at[3, b], left)))

    def x_end(b):
        xs[b][2].wait_recv()
        xs[b][3].wait_recv()

    ys = {}

    def y_start(blk, n):
        r = pa.at[blk, pl.ds(D + g * Q, Q)]
        ys[n] = [
            blk,
            start(rcopy(r, r, yss.at[0, n], yrs.at[0, n], right)),
            start(rcopy(r, r, yss.at[1, n], yrs.at[1, n], left)),
        ]

    def y_forward(n):
        blk = ys[n][0]
        ys[n][1].wait_recv()
        r = pa.at[blk, pl.ds(D + g_of(x + 3) * Q, Q // 2)]
        ys[n].append(start(rcopy(r, r, yss.at[2, n], yrs.at[2, n], right)))
        ys[n][2].wait_recv()
        r = pa.at[blk, pl.ds(D + g_of(x + 1) * Q + Q // 2, Q // 2)]
        ys[n].append(start(rcopy(r, r, yss.at[3, n], yrs.at[3, n], left)))

    def y_end(n):
        ys[n][3].wait_recv()
        ys[n][4].wait_recv()

    def attend(blk):
        def half(i, c):
            q = qr[blk, pl.ds(i * 4, 4)].reshape(256, DQ)
            s = nt(q, pa[blk])
            top = jnp.max(s, axis=1, keepdims=True)
            w = jnp.exp((s - top) * SCALE).astype(BF)
            total = jnp.sum(w.astype(F32), axis=1, keepdims=True)
            o = nn(w, pa[blk, :, :DL]) / total
            l = jnp.broadcast_to(top * SCALE + jnp.log(total), (256, 128))
            for n in range(4):
                at = pl.ds(pl.multiple_of((i * 4 + n) * 512 + blk * 64, 64), 64)
                for f in range(4):
                    lat[f, at, :] = o[n * 64 : n * 64 + 64, f * 128 : f * 128 + 128]
                lse[at, :] = l[n * 64 : n * 64 + 64]
            return c

        lax.fori_loop(0, 2, half, 0)

    for n in range(5):
        ring_start(0, 1, n)
        ring_start(1, 1, n)
        if n == 0:
            page_send(0)
        else:
            for m in range(7):
                query_send(n - 1, m)
    page_send(1)
    page_send(2)
    for t in range(1, 5):
        for n in range(5):
            for dirn in (0, 1):
                if n not in pieces(dirn, t):
                    continue
                rings[dirn, t, n].wait_recv()
                if t < 4 and n in pieces(dirn, t + 1):
                    ring_start(dirn, t + 1, n)
                if n == 0 and t < 4:
                    y_start((z - t + 8) % 8 if dirn == 0 else (z + t) % 8, 2 * t - 2 + dirn)
            if t == 4 and n == 0:
                y_start((z + 4) % 8, 6)
        if t < 3:
            page_send(2 * t + 1)
            page_send(2 * t + 2)
        if t == 3:
            page_send(7)
        if t > 1:
            y_forward(2 * t - 4)
            y_forward(2 * t - 3)
        if t == 1:
            own_w.wait()
            page_wait(0)
            x_start(0)
        if t == 2:
            page_wait(1)
            page_wait(2)
            x_start(1)
            x_start(2)
            x_forward(0)
        if t == 3:
            x_forward(1)
            x_forward(2)
    y_forward(6)
    page_wait(3)
    page_wait(4)
    x_start(3)
    x_start(4)
    own_q.wait()
    own_p.wait()
    for n in range(7):
        query_wait(n).wait_recv()
    attend(z)
    y_end(0)
    y_end(1)
    attend((z + 7) % 8)
    attend((z + 1) % 8)
    x_forward(3)
    x_forward(4)
    page_wait(5)
    page_wait(6)
    x_start(5)
    x_start(6)
    y_end(2)
    y_end(3)
    attend((z + 6) % 8)
    attend((z + 2) % 8)
    y_end(4)
    y_end(5)
    attend((z + 5) % 8)
    attend((z + 3) % 8)
    x_forward(5)
    x_forward(6)
    page_wait(7)
    x_start(7)
    y_end(6)
    attend((z + 4) % 8)

    lane = lax.broadcasted_iota(jnp.int32, (128, 128), 1)

    def project(h, c):
        rows = pl.ds(h, 128, stride=32)
        latent = jnp.concatenate([lat[f, rows, :] for f in range(4)], axis=1)
        outs[h] = nn(latent.astype(BF), vu[h]).astype(BF)
        return jnp.where(lane == h, lse[rows, :], c)

    lses[...] = lax.fori_loop(0, 32, project, jnp.zeros((128, 128), F32))

    back = []
    for n in range(7):
        dy, dc = DQDS[n]
        t = peer(dy, dc)
        there, here = pl.ds(t * 16, 16), pl.ds(yc * 16, 16)
        dev = (pre, z * 8 + t, rep)
        back.append(start(rcopy(outs.at[:, there], ret.at[:, here], bss.at[0, n], brs.at[0, n], dev)))
        back.append(start(rcopy(lses.at[there], rlse.at[here], bss.at[1, n], brs.at[1, n], dev)))
    here = pl.ds(yc * 16, 16)
    mine = [
        start(pltpu.make_async_copy(outs.at[:, here], ret.at[:, here], loc.at[3])),
        start(pltpu.make_async_copy(lses.at[here], rlse.at[here], loc.at[4])),
    ]
    x_forward(7)

    for b in range(8):
        x_end(b)
    for c in back:
        c.wait()
    for c in mine:
        c.wait()
    for n in range(7):
        query_wait(n).wait_send()
        for c in ys[n][1:]:
            c.wait_send()
    for c in rings.values():
        c.wait_send()
    for b in range(8):
        for c in xs[b]:
            c.wait_send()


def exchange(qs, pf, ps, vu):
    S = pltpu.SemaphoreType.DMA
    return pl.pallas_call(
        exchange_kernel,
        out_shape=(
            jax.ShapeDtypeStruct((64, 2, 4, 16, DQ), BF),
            jax.ShapeDtypeStruct((32, 128, 128), BF),
            jax.ShapeDtypeStruct((128, 128), F32),
        ),
        in_specs=[ANY, ANY, ANY, VM],
        out_specs=(ANY, ANY, ANY),
        scratch_shapes=[
            pltpu.VMEM((8, 8, 2, 32, DQ), BF),
            pltpu.VMEM((8, 1024, DQ), BF),
            pltpu.VMEM((4, 4096, 128), F32),
            pltpu.VMEM((4096, 128), F32),
            pltpu.VMEM((32, 128, 128), BF),
            pltpu.VMEM((128, 128), F32),
            S((7,)), S((7,)), S((2, 4, 5)), S((2, 4, 5)), S((8,)), S((8,)),
            S((4, 8)), S((4, 8)), S((4, 7)), S((4, 7)), S((2, 7)), S((2, 7)), S((5,)),
        ],
        compiler_params=pltpu.CompilerParams(
            collective_id=0, has_side_effects=True, vmem_limit_bytes=56 * 2**20
        ),
    )(qs, pf, ps, vu)


def local_kernel(
    req, length, q, suffix, slen, pages, vu, slot, ret, rlse, out, acc, top, tot
):
    step = pl.program_id(0)

    @pl.when(step == 0)
    def _():
        acc[...] = jnp.zeros_like(acc)
        tot[...] = jnp.zeros_like(tot)
        top[...] = jnp.full_like(top, NEG)

    def merge(r, m, l, o):
        at = pl.ds(pl.multiple_of(r * 32, 32), 32)
        old = top[at, :1]
        new = jnp.maximum(old, m)
        a, b = jnp.exp(old - new), jnp.exp(m - new)
        for f in range(4):
            acc[f, at, :] = acc[f, at, :] * a + o[:, f * 128 : f * 128 + 128] * b
        tot[at, :] = tot[at, :] * a + l * b
        top[at, :] = jnp.broadcast_to(new, (32, 128))

    def block(queried, keys, span, lens, count):
        rows, cols = count * 32, count * span
        r = lax.broadcasted_iota(jnp.int32, (rows, 1), 0) // 32
        limit = jnp.zeros((rows, 1), jnp.int32)
        for n in range(count):
            limit = jnp.where(r == n, lens[n], limit)
        c = lax.broadcasted_iota(jnp.int32, (rows, cols), 1) - r * span
        ok = (c >= 0) & (c < limit)
        s = jnp.where(ok, nt(queried, keys) * SCALE, NEG)
        m = jnp.max(s, axis=1, keepdims=True)
        w = jnp.where(ok, jnp.exp(s - m), 0.0).astype(BF)
        l = jnp.sum(w.astype(F32), axis=1, keepdims=True)
        return m, l, nn(w, keys[:, :DL])

    first = step * 8
    queried = q[pl.ds(first, 8)].reshape(256, DQ)
    m, l, o = block(queried, suffix[...].reshape(256, DQ), 32, [slen[first + n] for n in range(8)], 8)
    for n in range(8):
        at = slice(n * 32, n * 32 + 32)
        merge(first + n, m[at], l[at], o[at])

    for k in range(4):
        s0 = step * 16 + k * 4
        owners = [req[s0 + n] for n in range(4)]
        queried = jnp.concatenate([q[r] for r in owners], axis=0)
        keys = pages[k * 4 : k * 4 + 4].reshape(256, DQ)
        m, l, o = block(queried, keys, 64, [length[s0 + n] for n in range(4)], 4)
        for n in range(4):
            at = slice(n * 32, n * 32 + 32)
            merge(owners[n], m[at], l[at], o[at])

    @pl.when(step == pl.num_programs(0) - 1)
    def _():
        hot = lax.broadcasted_iota(jnp.int32, (64, 128), 1) == slot[...]
        pick = hot.astype(BF)
        plse = jnp.dot(hot.astype(F32), rlse[...], precision=lax.Precision.HIGHEST, preferred_element_type=F32)
        lane = lax.broadcasted_iota(jnp.int32, (64, 128), 1)

        def head(h, c):
            rows = pl.ds(h, 64, stride=32)
            lsep = jnp.sum(jnp.where(lane == h, plse, 0.0), axis=1, keepdims=True)
            total = tot[rows, :][:, :1]
            lser = top[rows, :][:, :1] + jnp.log(total)
            high = jnp.maximum(lsep, lser)
            ep, er = jnp.exp(lsep - high), jnp.exp(lser - high)
            latent = jnp.concatenate([acc[f, rows, :] for f in range(4)], axis=1)
            here = nn((latent / total).astype(BF), vu[h])
            there = nn(pick, ret[h])
            out[:, pl.ds(pl.multiple_of(h * 128, 128), 128)] = ((ep * there + er * here) / (ep + er)).astype(BF)
            return c

        lax.fori_loop(0, 32, head, 0, unroll=4)


def local(req, length, q, suffix, slen, pages, vu, slot, ret, rlse):
    def whole(shape):
        return pl.BlockSpec(shape, lambda *a: (0,) * len(shape))

    return pl.pallas_call(
        local_kernel,
        grid=(8,),
        out_shape=jax.ShapeDtypeStruct((64, 4096), BF),
        in_specs=[
            SM, SM,
            whole((64, 32, DQ)),
            pl.BlockSpec((8, 32, DQ), lambda i: (i, 0, 0)),
            SM,
            pl.BlockSpec((16, 64, DQ), lambda i: (i, 0, 0)),
            whole((32, DL, 128)),
            whole((64, 1)),
            whole((32, 128, 128)),
            whole((128, 128)),
        ],
        out_specs=whole((64, 4096)),
        scratch_shapes=[
            pltpu.VMEM((4, 2048, 128), F32),
            pltpu.VMEM((2048, 128), F32),
            pltpu.VMEM((2048, 128), F32),
        ],
        compiler_params=pltpu.CompilerParams(vmem_limit_bytes=56 * 2**20),
    )(req, length, q, suffix, slen, pages, vu, slot, ret, rlse)


def per_device(
    queries, prefix_of, prefix_cache, suffix_cache, suffix_len, fresh_pages,
    page_owner, page_request, page_tokens, value_up,
):
    dec = lax.axis_index("dec")
    qs, ps, slot = bucket(prefix_of[:, 0], page_owner[:, 0], queries, fresh_pages)
    W, ret, rlse = exchange(qs, prefix_cache[0], ps, value_up)

    mine = page_owner[:, 0].reshape(64, 64) == dec
    nth = jnp.cumsum(mine.astype(jnp.int32), axis=1)
    pick = mine[:, None, :] & (nth[:, None, :] == jnp.arange(1, 3)[None, :, None])
    req = jnp.sum(jnp.where(pick, page_request.reshape(64, 1, 64), 0), axis=2).reshape(128)
    length = jnp.sum(jnp.where(pick, page_tokens.reshape(64, 1, 64), 0), axis=2).reshape(128)
    return local(
        req, length, queries, suffix_cache, suffix_len, W.reshape(128, 64, DQ), value_up,
        slot.reshape(64, 1), ret, rlse,
    )


def solution(mesh):
    heads = ("pre", "rep")
    placed = (
        P("dec", heads, None),
        P("dec", None),
        P("dec", None, None),
        P("dec", None, None),
        P("dec"),
        P("dec", heads, None),
        P(),
        P(),
        P(),
        P(heads, None, None),
    )
    return jax.shard_map(
        per_device, mesh=mesh, in_specs=placed, out_specs=P("dec", heads), check_vma=False
    )
```

```python
import functools

import jax
import jax.numpy as jnp
from jax import lax
from jax.experimental import pallas as pl
from jax.experimental.pallas import tpu as pltpu
from jax.sharding import PartitionSpec as P

MESH = pl.DeviceIdType.MESH
BF, F32 = jnp.bfloat16, jnp.float32
ANY = pl.BlockSpec(memory_space=pl.ANY)
VM = pl.BlockSpec(memory_space=pltpu.VMEM)
SM = pl.BlockSpec(memory_space=pltpu.SMEM)
DL, DQ = 512, 576
DP = 1152
SCALE = 192.0**-0.5
NEG = -1e30
ORDER = (0, 1, -1, 2, -2, 3, -3, 4)
PLAN = ((0, 1, 2), (3, 4), (5, 6), (7,))
D, Q = 256, 64
PIECE = 64
DQDS = (((1, 0)), ((-1, 0)), ((1, 1)), ((-1, 1)), ((2, 0)), ((2, 1)), ((0, 1)))


def bucket_kernel(
    pref, owner, q_hbm, f_hbm, p_hbm, qs_hbm, ps_hbm, pp_hbm, slot, count, queries, fresh, prefix, qs, ps, pp, sem
):
    dec = lax.axis_index("dec")
    loads = [
        pltpu.make_async_copy(p_hbm, prefix, sem.at[0]),
        pltpu.make_async_copy(f_hbm, fresh, sem.at[1]),
        pltpu.make_async_copy(q_hbm, queries, sem.at[2]),
    ]
    stores = [
        pltpu.make_async_copy(pp, pp_hbm, sem.at[3]),
        pltpu.make_async_copy(ps, ps_hbm, sem.at[4]),
        pltpu.make_async_copy(qs, qs_hbm, sem.at[5]),
    ]
    for c in loads:
        c.start()
    qs[...] = jnp.zeros_like(qs)
    ps[...] = jnp.zeros_like(ps)

    def clear(i, c):
        count[0, i] = 0
        count[1, i] = 0
        return c

    lax.fori_loop(0, 64, clear, 0, unroll=8)
    half = lax.broadcasted_iota(jnp.int32, (16, 128), 1) // 64
    loads[0].wait()
    pp[:, :DL] = prefix[:512, :DL]
    pp[:, DL : 2 * DL] = prefix[512:, :DL]
    pp[:, 2 * DL :] = jnp.concatenate([prefix[:512, DL:], prefix[512:, DL:]], axis=1)
    stores[0].start()

    def put_page(i, c):
        o = owner[dec * 64 + i]
        k = count[1, o]
        count[1, o] = k + 1
        page = fresh[i]
        ps[o, :, pl.ds(pl.multiple_of(k * DL, DL), DL)] = page[:, :DL]
        rotary = page[:, DL:].astype(F32)
        both = jnp.concatenate([rotary, rotary], axis=1)
        ps[o, :, 2 * DL :] = jnp.where(half == k, both, ps[o, :, 2 * DL :].astype(F32)).astype(BF)
        return c

    def put_query(i, c):
        p = pref[i]
        k = count[0, p]
        count[0, p] = k + 1
        to = (p % 8) * 16 + (p // 8) * 2 + k
        qs[to] = queries[i]
        slot[i] = to
        return c

    loads[1].wait()
    lax.fori_loop(0, 64, put_page, 0)
    stores[1].start()
    loads[2].wait()
    lax.fori_loop(0, 64, put_query, 0)
    stores[2].start()
    for c in stores:
        c.wait()


def bucket(pref, owner, queries, fresh, prefix):
    qs, ps, pp, slot = pl.pallas_call(
        bucket_kernel,
        out_shape=(
            jax.ShapeDtypeStruct((128, 32, DQ), BF),
            jax.ShapeDtypeStruct((64, 16, DP), BF),
            jax.ShapeDtypeStruct((512, DP), BF),
            jax.ShapeDtypeStruct((64,), jnp.int32),
        ),
        in_specs=[SM, SM, ANY, ANY, ANY],
        out_specs=(ANY, ANY, ANY, SM),
        scratch_shapes=[
            pltpu.SMEM((2, 64), jnp.int32),
            pltpu.VMEM((64, 32, DQ), BF),
            pltpu.VMEM((64, 16, DQ), BF),
            pltpu.VMEM((1024, DQ), BF),
            pltpu.VMEM((128, 32, DQ), BF),
            pltpu.VMEM((64, 16, DP), BF),
            pltpu.VMEM((512, DP), BF),
            pltpu.SemaphoreType.DMA((6,)),
        ],
        compiler_params=pltpu.CompilerParams(vmem_limit_bytes=60 * 2**20),
    )(pref, owner, queries, fresh, prefix)
    return qs.reshape(8, 8, 2, 32, DQ), ps, pp, slot


def rcopy(src, dst, ss, rs, dev):
    return pltpu.make_async_remote_copy(
        src_ref=src, dst_ref=dst, send_sem=ss, recv_sem=rs, device_id=dev, device_id_type=MESH
    )


def nt(a, b):
    return lax.dot_general(a, b, (((1,), (1,)), ((), ())), preferred_element_type=F32)


def nn(a, b):
    return jnp.dot(a, b, preferred_element_type=F32)


def pad_rotary(q, k):
    r = q[:, DL:]
    zero = jnp.zeros_like(r)
    return jnp.concatenate([zero, r] if k else [r, zero], axis=1)


def exchange_kernel(
    req, length, slen, qs, pf, ps, q_hbm, suffix_hbm, vu_hbm, slot, member, out,
    W, qr, pa, lat, lse, latr, lser, outs, lses, ret, rlse, q, suffix, vu,
    qss, qrs, rss, rrs, pss, prs, xss, xrs, yss, yrs, bss, brs, loc,
):
    pre, dec, rep = lax.axis_index("pre"), lax.axis_index("dec"), lax.axis_index("rep")
    z, y, core = dec // 8, (dec // 2) % 4, dec % 2
    yc = dec % 8
    x = rep * 2 + pre
    g = pre * 2 + rep

    def at_x(v):
        v = v % 4
        return (v % 2, dec, v // 2)

    def g_of(v):
        v = v % 4
        return (v % 2) * 2 + v // 2

    right, left = at_x(x + 1), at_x(x + 3)
    bar = pltpu.get_barrier_semaphore()

    def hello(o, c):
        pl.semaphore_signal(bar, inc=1, device_id=(pre, (dec + o) % 64, rep), device_id_type=MESH)
        return c

    lax.fori_loop(1, 64, hello, 0)
    pl.semaphore_signal(bar, inc=1, device_id=right, device_id_type=MESH)
    pl.semaphore_signal(bar, inc=1, device_id=left, device_id_type=MESH)
    pl.semaphore_wait(bar, 65)

    def start(c):
        c.start()
        return c

    own_q = start(pltpu.make_async_copy(qs.at[yc], qr.at[:, yc], loc.at[0]))
    own_p = start(pltpu.make_async_copy(pf, pa.at[z], loc.at[1]))
    own_w = start(pltpu.make_async_copy(ps.at[dec], W.at[dec, g], loc.at[2]))
    loads = [
        start(pltpu.make_async_copy(q_hbm, q, loc.at[5])),
        start(pltpu.make_async_copy(suffix_hbm, suffix, loc.at[6])),
        start(pltpu.make_async_copy(vu_hbm, vu, loc.at[7])),
    ]

    def peer(dy, dc):
        return ((y + dy + 4) % 4) * 2 + (core + dc) % 2

    def query_send(j, n):
        dy, dc = DQDS[n]
        t = peer(dy, dc)
        part = pl.ds(2 * j, 2)
        return start(rcopy(qs.at[t, part], qr.at[part, yc], qss.at[n], qrs.at[n], (pre, z * 8 + t, rep)))

    def query_wait(n):
        dy, dc = DQDS[n]
        s = peer(-dy, dc)
        return rcopy(qs.at[0], qr.at[:, s], qss.at[n], qrs.at[n], (pre, z * 8 + s, rep))

    def zdev(dz):
        return (pre, ((z + dz + 8) % 8) * 8 + yc, rep)

    def piece(n, last, dirn):
        if n == 0:
            return pl.ds(D + g * Q + dirn * (Q // 2), Q // 2) if last else pl.ds(D + g * Q, Q)
        return pl.ds((n - 1) * PIECE, PIECE)

    def pieces(dirn, t):
        if t < 4:
            return (0, 1, 2, 3, 4)
        return (0, 1, 2) if dirn == 0 else (0, 3, 4)

    rings = {}

    def ring_start(dirn, t, n):
        sgn = 1 - 2 * dirn
        blk = (z - sgn * (t - 1) + 8) % 8
        rows = piece(n, t == 4, dirn)
        src = pf.at[rows] if t == 1 else pa.at[blk, rows]
        rings[dirn, t, n] = start(
            rcopy(src, pa.at[blk, rows], rss.at[dirn, t - 1, n], rrs.at[dirn, t - 1, n], zdev(sgn))
        )

    def page_send(b):
        dz = ORDER[b]

        def one(o, c):
            t = ((z + dz + 8) % 8) * 8 + (yc + o) % 8
            rcopy(ps.at[t], W.at[dec, g], pss.at[b], prs.at[b], (pre, t, rep)).start()
            return c

        lax.fori_loop(1 if dz == 0 else 0, 8, one, 0)

    def batch(b, first=0, count=8):
        return pl.ds(((z - ORDER[b] + 8) % 8) * 8 + first, count)

    def page_wait(b):
        w = W.at[pl.ds(0, 7 if ORDER[b] == 0 else 8), 0]
        c = rcopy(w, w, pss.at[b], prs.at[b], right)
        c.wait_send()
        c.wait_recv()

    xs = {}

    def x_start(b):
        r = W.at[batch(b), g]
        xs[b] = [
            start(rcopy(r, r, xss.at[0, b], xrs.at[0, b], right)),
            start(rcopy(r, r, xss.at[1, b], xrs.at[1, b], left)),
        ]

    def x_forward(b):
        xs[b][0].wait_recv()
        r = W.at[batch(b, 0, 4), g_of(x + 3)]
        xs[b].append(start(rcopy(r, r, xss.at[2, b], xrs.at[2, b], right)))
        xs[b][1].wait_recv()
        r = W.at[batch(b, 4, 4), g_of(x + 1)]
        xs[b].append(start(rcopy(r, r, xss.at[3, b], xrs.at[3, b], left)))

    def x_end(b):
        xs[b][2].wait_recv()
        xs[b][3].wait_recv()

    ys = {}

    def y_start(blk, n):
        r = pa.at[blk, pl.ds(D + g * Q, Q)]
        ys[n] = [
            blk,
            start(rcopy(r, r, yss.at[0, n], yrs.at[0, n], right)),
            start(rcopy(r, r, yss.at[1, n], yrs.at[1, n], left)),
        ]

    def y_forward(n):
        blk = ys[n][0]
        ys[n][1].wait_recv()
        r = pa.at[blk, pl.ds(D + g_of(x + 3) * Q, Q // 2)]
        ys[n].append(start(rcopy(r, r, yss.at[2, n], yrs.at[2, n], right)))
        ys[n][2].wait_recv()
        r = pa.at[blk, pl.ds(D + g_of(x + 1) * Q + Q // 2, Q // 2)]
        ys[n].append(start(rcopy(r, r, yss.at[3, n], yrs.at[3, n], left)))

    def y_end(n):
        ys[n][3].wait_recv()
        ys[n][4].wait_recv()

    def keep(to_lat, to_lse, at, o, l):
        for f in range(4):
            to_lat[f, at, :] = o[:, f * 128 : f * 128 + 128]
        to_lse[at, :] = jnp.broadcast_to(l, (l.shape[0], 128))

    def attend(blk):
        def half(i, c):
            queried = qr[blk, pl.ds(i * 4, 4)].reshape(256, DQ)
            head = queried[:, :DL]
            tail = pa[blk, :, 2 * DL :]
            s0 = nt(head, pa[blk, :, :DL]) + nt(pad_rotary(queried, 0), tail)
            s1 = nt(head, pa[blk, :, DL : 2 * DL]) + nt(pad_rotary(queried, 1), tail)
            top = jnp.maximum(jnp.max(s0, axis=1, keepdims=True), jnp.max(s1, axis=1, keepdims=True))
            w0 = jnp.exp((s0 - top) * SCALE).astype(BF)
            w1 = jnp.exp((s1 - top) * SCALE).astype(BF)
            total = jnp.sum(w0.astype(F32), axis=1, keepdims=True) + jnp.sum(w1.astype(F32), axis=1, keepdims=True)
            o = (nn(w0, pa[blk, :, :DL]) + nn(w1, pa[blk, :, DL : 2 * DL])) / total
            l = top * SCALE + jnp.log(total)
            for n in range(4):
                at = pl.ds(pl.multiple_of((i * 4 + n) * 512 + blk * 64, 64), 64)
                part = slice(n * 64, n * 64 + 64)
                keep(lat, lse, at, o[part], l[part])
            return c

        lax.fori_loop(0, 2, half, 0)

    def masked(s, w_keys, span, lens):
        count = len(lens)
        rows, cols = count * 32, count * span
        r = lax.broadcasted_iota(jnp.int32, (rows, 1), 0) // 32
        limit = jnp.zeros((rows, 1), jnp.int32)
        for n in range(count):
            limit = jnp.where(r == n, lens[n], limit)
        c = lax.broadcasted_iota(jnp.int32, (rows, cols), 1) - r * span
        ok = (c >= 0) & (c < limit)
        s = jnp.where(ok, s * SCALE, NEG)
        m = jnp.max(s, axis=1, keepdims=True)
        w = jnp.where(ok, jnp.exp(s - m), 0.0).astype(BF)
        l = jnp.sum(w.astype(F32), axis=1, keepdims=True)
        l = jnp.where(l > 0.0, l, 1.0)
        return nn(w, w_keys) / l, m + jnp.log(l)

    def resident(i):
        queried = q[pl.ds(i * 8, 8)].reshape(256, DQ)
        keys = suffix[pl.ds(i * 8, 8)].reshape(256, DQ)
        o, l = masked(nt(queried, keys), keys[:, :DL], 32, [slen[i * 8 + n] for n in range(8)])
        keep(latr, lser, pl.ds(pl.multiple_of(i * 256, 256), 256), o, l)

    def residents(i, j):
        def one(n, c):
            resident(n)
            return c

        lax.fori_loop(i, j, one, 0)

    def page_attend(b):
        base = ((z - ORDER[b] + 8) % 8) * 8

        def one(i, c):
            src = base + i * 4
            tail = W[pl.ds(src, 4), :, :, 2 * DL :].reshape(256, 128)
            for k in range(2):
                slots = [(src + n) * 2 + k for n in range(4)]
                queried = jnp.concatenate([q[req[v]] for v in slots], axis=0)
                keys = W[pl.ds(src, 4), :, :, k * DL : k * DL + DL].reshape(256, DL)
                s = nt(queried[:, :DL], keys) + nt(pad_rotary(queried, k), tail)
                o, l = masked(s, keys, 64, [length[v] for v in slots])
                for n in range(4):
                    part = slice(n * 32, n * 32 + 32)
                    keep(lat, lse, pl.ds(pl.multiple_of(slots[n] * 32, 32), 32), o[part], l[part])
            return c

        lax.fori_loop(0, 2, one, 0)

    def gathered(ref, rows):
        return jnp.concatenate([ref[f, rows, :] for f in range(4)], axis=1).astype(BF)

    lane = lax.broadcasted_iota(jnp.int32, (128, 128), 1)

    for n in range(5):
        ring_start(0, 1, n)
        ring_start(1, 1, n)
        if n == 0:
            for b in PLAN[0]:
                page_send(b)
        else:
            for m in range(7):
                query_send(n - 1, m)
    loads[0].wait()
    loads[1].wait()
    for t in range(1, 5):
        residents(2 * t - 2, 2 * t)
        for n in range(5):
            for dirn in (0, 1):
                if n not in pieces(dirn, t):
                    continue
                rings[dirn, t, n].wait_recv()
                if t < 4 and n in pieces(dirn, t + 1):
                    ring_start(dirn, t + 1, n)
                if n == 0 and t < 4:
                    y_start((z - t + 8) % 8 if dirn == 0 else (z + t) % 8, 2 * t - 2 + dirn)
            if t == 4 and n == 0:
                y_start((z + 4) % 8, 6)
        if t < 4:
            for b in PLAN[t]:
                page_send(b)
        if t == 1:
            own_w.wait()
        for b in PLAN[t - 1]:
            page_wait(b)
            x_start(b)
        if t == 4:
            y_forward(6)
        else:
            y_forward(2 * t - 2)
            y_forward(2 * t - 1)
        if t < 4:
            for b in PLAN[t - 1]:
                x_forward(b)
    own_q.wait()
    own_p.wait()
    for n in range(7):
        query_wait(n).wait_recv()
    attend(z)
    y_end(0)
    y_end(1)
    attend((z + 7) % 8)
    attend((z + 1) % 8)
    y_end(2)
    y_end(3)
    attend((z + 6) % 8)
    attend((z + 2) % 8)
    for b in PLAN[3]:
        x_forward(b)
    y_end(4)
    y_end(5)
    attend((z + 5) % 8)
    attend((z + 3) % 8)
    y_end(6)
    attend((z + 4) % 8)
    loads[2].wait()

    def project(h, c):
        rows = pl.ds(h, 128, stride=32)
        outs[h] = nn(gathered(lat, rows), vu[h]).astype(BF)
        return jnp.where(lane == h, lse[rows, :], c)

    lses[...] = lax.fori_loop(0, 32, project, jnp.zeros((128, 128), F32), unroll=2)

    back = []
    for n in range(7):
        dy, dc = DQDS[n]
        t = peer(dy, dc)
        there, here = pl.ds(t * 16, 16), pl.ds(yc * 16, 16)
        dev = (pre, z * 8 + t, rep)
        back.append(start(rcopy(outs.at[:, there], ret.at[:, here], bss.at[0, n], brs.at[0, n], dev)))
        back.append(start(rcopy(lses.at[there], rlse.at[here], bss.at[1, n], brs.at[1, n], dev)))
    here = pl.ds(yc * 16, 16)
    mine = [
        start(pltpu.make_async_copy(outs.at[:, here], ret.at[:, here], loc.at[3])),
        start(pltpu.make_async_copy(lses.at[here], rlse.at[here], loc.at[4])),
    ]

    for b in range(8):
        x_end(b)
        page_attend(b)

    for c in back:
        c.wait()
    for c in mine:
        c.wait()

    def column(h, c):
        return jnp.where(lane == h, lse[pl.ds(h, 128, stride=32), :], c)

    lses[...] = jnp.transpose(lax.fori_loop(0, 32, column, jnp.zeros((128, 128), F32)))
    hot = lax.broadcasted_iota(jnp.int32, (64, 128), 1) == slot[...]
    pick = hot.astype(BF)
    mem = lax.broadcasted_iota(jnp.int32, (64, 128), 0) == member[...]
    plse = jnp.dot(hot.astype(F32), rlse[...], precision=lax.Precision.HIGHEST, preferred_element_type=F32)

    def finish(h, c):
        rows = pl.ds(h, 64, stride=32)
        lp = jnp.sum(jnp.where(lane[:64] == h, plse, 0.0), axis=1, keepdims=True)
        lr = lser[rows, :][:, :1]
        lw = jnp.where(mem, lses[pl.ds(h, 1), :], NEG)
        high = jnp.maximum(jnp.maximum(lp, lr), jnp.max(lw, axis=1, keepdims=True))
        wp, wr = jnp.exp(lp - high), jnp.exp(lr - high)
        ww = jnp.where(mem, jnp.exp(lw - high), 0.0).astype(BF)
        below = wp + wr + jnp.sum(ww.astype(F32), axis=1, keepdims=True)
        v = vu[h]
        paged = nn(ww, nn(gathered(lat, pl.ds(h, 128, stride=32)), v).astype(BF))
        total = wp * nn(pick, ret[h]) + wr * nn(gathered(latr, rows), v) + paged
        out[:, pl.ds(pl.multiple_of(h * 128, 128), 128)] = (total / below).astype(BF)
        return c

    lax.fori_loop(0, 32, finish, 0, unroll=4)

    for n in range(7):
        query_wait(n).wait_send()
        for c in ys[n][1:]:
            c.wait_send()
    for c in rings.values():
        c.wait_send()
    for b in range(8):
        for c in xs[b]:
            c.wait_send()


def exchange(req, length, slen, qs, pf, ps, q, suffix, vu, slot, member):
    S = pltpu.SemaphoreType.DMA
    return pl.pallas_call(
        exchange_kernel,
        out_shape=jax.ShapeDtypeStruct((64, 4096), BF),
        in_specs=[SM, SM, SM] + [ANY] * 6 + [VM, VM],
        out_specs=VM,
        scratch_shapes=[
            pltpu.VMEM((64, 4, 16, DP), BF),
            pltpu.VMEM((8, 8, 2, 32, DQ), BF),
            pltpu.VMEM((8, 512, DP), BF),
            pltpu.VMEM((4, 4096, 128), F32),
            pltpu.VMEM((4096, 128), F32),
            pltpu.VMEM((4, 2048, 128), F32),
            pltpu.VMEM((2048, 128), F32),
            pltpu.VMEM((32, 128, 128), BF),
            pltpu.VMEM((128, 128), F32),
            pltpu.VMEM((32, 128, 128), BF),
            pltpu.VMEM((128, 128), F32),
            pltpu.VMEM((64, 32, DQ), BF),
            pltpu.VMEM((64, 32, DQ), BF),
            pltpu.VMEM((32, DL, 128), BF),
            S((7,)), S((7,)), S((2, 4, 5)), S((2, 4, 5)), S((8,)), S((8,)),
            S((4, 8)), S((4, 8)), S((4, 7)), S((4, 7)), S((2, 7)), S((2, 7)), S((8,)),
        ],
        compiler_params=pltpu.CompilerParams(
            collective_id=0, has_side_effects=True, vmem_limit_bytes=60 * 2**20
        ),
    )(req, length, slen, qs, pf, ps, q, suffix, vu, slot, member)


def per_device(
    queries, prefix_of, prefix_cache, suffix_cache, suffix_len, fresh_pages,
    page_owner, page_request, page_tokens, value_up,
):
    dec = lax.axis_index("dec")
    qs, ps, pp, slot = bucket(prefix_of[:, 0], page_owner[:, 0], queries, fresh_pages, prefix_cache[0])

    mine = page_owner[:, 0].reshape(64, 64) == dec
    nth = jnp.cumsum(mine.astype(jnp.int32), axis=1)
    pick = mine[:, None, :] & (nth[:, None, :] == jnp.arange(1, 3)[None, :, None])
    req = jnp.sum(jnp.where(pick, page_request.reshape(64, 1, 64), 0), axis=2).reshape(128)
    length = jnp.sum(jnp.where(pick, page_tokens.reshape(64, 1, 64), 0), axis=2).reshape(128)
    member = jnp.where(length > 0, req, -1).reshape(1, 128)
    return exchange(
        req, length, suffix_len, qs, pp, ps, queries, suffix_cache, value_up,
        slot.reshape(64, 1), member,
    )


def solution(mesh):
    heads = ("pre", "rep")
    placed = (
        P("dec", heads, None),
        P("dec", None),
        P("dec", None, None),
        P("dec", None, None),
        P("dec"),
        P("dec", heads, None),
        P(),
        P(),
        P(),
        P(heads, None, None),
    )
    return jax.shard_map(
        per_device, mesh=mesh, in_specs=placed, out_specs=P("dec", heads), check_vma=False
    )
```

```python
import functools

import jax
import jax.numpy as jnp
from jax import lax
from jax.experimental import pallas as pl
from jax.experimental.pallas import tpu as pltpu
from jax.sharding import PartitionSpec as P

MESH = pl.DeviceIdType.MESH
BF, F32 = jnp.bfloat16, jnp.float32
ANY = pl.BlockSpec(memory_space=pl.ANY)
VM = pl.BlockSpec(memory_space=pltpu.VMEM)
SM = pl.BlockSpec(memory_space=pltpu.SMEM)
DL, DQ = 512, 576
DP = 1152
SCALE = 192.0**-0.5
NEG = -1e30
ORDER = (0, 1, -1, 2, -2, 3, -3, 4)
PLAN = ((0, 1, 2), (3, 4), (5, 6), (7,))
D, Q = 256, 64
PIECE = 64
DQDS = (((1, 0)), ((-1, 0)), ((1, 1)), ((-1, 1)), ((2, 0)), ((2, 1)), ((0, 1)))


def bucket_kernel(
    pref, owner, q_hbm, f_hbm, p_hbm, qs_hbm, ps_hbm, pp_hbm, slot, count, queries, fresh, prefix, qs, ps, pp, sem
):
    dec = lax.axis_index("dec")
    loads = [
        pltpu.make_async_copy(p_hbm, prefix, sem.at[0]),
        pltpu.make_async_copy(f_hbm, fresh, sem.at[1]),
        pltpu.make_async_copy(q_hbm, queries, sem.at[2]),
    ]
    stores = [
        pltpu.make_async_copy(pp, pp_hbm, sem.at[3]),
        pltpu.make_async_copy(ps, ps_hbm, sem.at[4]),
        pltpu.make_async_copy(qs, qs_hbm, sem.at[5]),
    ]
    for c in loads:
        c.start()
    qs[...] = jnp.zeros_like(qs)
    ps[...] = jnp.zeros_like(ps)

    def clear(i, c):
        count[0, i] = 0
        count[1, i] = 0
        return c

    lax.fori_loop(0, 64, clear, 0, unroll=8)
    half = lax.broadcasted_iota(jnp.int32, (16, 128), 1) // 64
    loads[0].wait()
    pp[:, :DL] = prefix[:512, :DL]
    pp[:, DL : 2 * DL] = prefix[512:, :DL]
    pp[:, 2 * DL :] = jnp.concatenate([prefix[:512, DL:], prefix[512:, DL:]], axis=1)
    stores[0].start()

    def put_page(i, c):
        o = owner[dec * 64 + i]
        k = count[1, o]
        count[1, o] = k + 1
        page = fresh[i]
        ps[o, :, pl.ds(pl.multiple_of(k * DL, DL), DL)] = page[:, :DL]
        rotary = page[:, DL:].astype(F32)
        both = jnp.concatenate([rotary, rotary], axis=1)
        ps[o, :, 2 * DL :] = jnp.where(half == k, both, ps[o, :, 2 * DL :].astype(F32)).astype(BF)
        return c

    def put_query(i, c):
        p = pref[i]
        k = count[0, p]
        count[0, p] = k + 1
        to = (p % 8) * 16 + (p // 8) * 2 + k
        qs[to] = queries[i]
        slot[i] = to
        return c

    loads[1].wait()
    lax.fori_loop(0, 64, put_page, 0)
    stores[1].start()
    loads[2].wait()
    lax.fori_loop(0, 64, put_query, 0)
    stores[2].start()
    for c in stores:
        c.wait()


def bucket(pref, owner, queries, fresh, prefix):
    qs, ps, pp, slot = pl.pallas_call(
        bucket_kernel,
        out_shape=(
            jax.ShapeDtypeStruct((128, 32, DQ), BF),
            jax.ShapeDtypeStruct((64, 16, DP), BF),
            jax.ShapeDtypeStruct((512, DP), BF),
            jax.ShapeDtypeStruct((64,), jnp.int32),
        ),
        in_specs=[SM, SM, ANY, ANY, ANY],
        out_specs=(ANY, ANY, ANY, SM),
        scratch_shapes=[
            pltpu.SMEM((2, 64), jnp.int32),
            pltpu.VMEM((64, 32, DQ), BF),
            pltpu.VMEM((64, 16, DQ), BF),
            pltpu.VMEM((1024, DQ), BF),
            pltpu.VMEM((128, 32, DQ), BF),
            pltpu.VMEM((64, 16, DP), BF),
            pltpu.VMEM((512, DP), BF),
            pltpu.SemaphoreType.DMA((6,)),
        ],
        compiler_params=pltpu.CompilerParams(vmem_limit_bytes=60 * 2**20),
    )(pref, owner, queries, fresh, prefix)
    return qs.reshape(8, 8, 2, 32, DQ), ps, pp, slot


def rcopy(src, dst, ss, rs, dev):
    return pltpu.make_async_remote_copy(
        src_ref=src, dst_ref=dst, send_sem=ss, recv_sem=rs, device_id=dev, device_id_type=MESH
    )


def nt(a, b):
    return lax.dot_general(a, b, (((1,), (1,)), ((), ())), preferred_element_type=F32)


def nn(a, b):
    return jnp.dot(a, b, preferred_element_type=F32)


def pad_rotary(q, k):
    r = q[:, DL:]
    zero = jnp.zeros_like(r)
    return jnp.concatenate([zero, r] if k else [r, zero], axis=1)


def exchange_kernel(
    req, length, slen, qs, pf, ps, q_hbm, suffix_hbm, vu_hbm, slot, member, out,
    W, qr, pa, lat, lse, latr, lser, outs, lses, ret, rlse, q, suffix, vu,
    qss, qrs, rss, rrs, pss, prs, xss, xrs, yss, yrs, bss, brs, loc,
):
    pre, dec, rep = lax.axis_index("pre"), lax.axis_index("dec"), lax.axis_index("rep")
    z, y, core = dec // 8, (dec // 2) % 4, dec % 2
    yc = dec % 8
    x = rep * 2 + pre
    g = pre * 2 + rep

    def at_x(v):
        v = v % 4
        return (v % 2, dec, v // 2)

    def g_of(v):
        v = v % 4
        return (v % 2) * 2 + v // 2

    right, left = at_x(x + 1), at_x(x + 3)
    bar = pltpu.get_barrier_semaphore()

    def hello(o, c):
        pl.semaphore_signal(bar, inc=1, device_id=(pre, (dec + o) % 64, rep), device_id_type=MESH)
        return c

    lax.fori_loop(1, 64, hello, 0)
    pl.semaphore_signal(bar, inc=1, device_id=right, device_id_type=MESH)
    pl.semaphore_signal(bar, inc=1, device_id=left, device_id_type=MESH)
    pl.semaphore_wait(bar, 65)

    def start(c):
        c.start()
        return c

    own_q = start(pltpu.make_async_copy(qs.at[yc], qr.at[:, yc], loc.at[0]))
    own_p = start(pltpu.make_async_copy(pf, pa.at[z], loc.at[1]))
    own_w = start(pltpu.make_async_copy(ps.at[dec], W.at[dec, g], loc.at[2]))
    loads = [
        start(pltpu.make_async_copy(q_hbm, q, loc.at[5])),
        start(pltpu.make_async_copy(suffix_hbm, suffix, loc.at[6])),
        start(pltpu.make_async_copy(vu_hbm, vu, loc.at[7])),
    ]

    def peer(dy, dc):
        return ((y + dy + 4) % 4) * 2 + (core + dc) % 2

    def query_send(j, n):
        dy, dc = DQDS[n]
        t = peer(dy, dc)
        part = pl.ds(2 * j, 2)
        return start(rcopy(qs.at[t, part], qr.at[part, yc], qss.at[n], qrs.at[n], (pre, z * 8 + t, rep)))

    def query_wait(n):
        dy, dc = DQDS[n]
        s = peer(-dy, dc)
        return rcopy(qs.at[0], qr.at[:, s], qss.at[n], qrs.at[n], (pre, z * 8 + s, rep))

    def zdev(dz):
        return (pre, ((z + dz + 8) % 8) * 8 + yc, rep)

    def piece(n, last, dirn):
        if n == 0:
            return pl.ds(D + g * Q + dirn * (Q // 2), Q // 2) if last else pl.ds(D + g * Q, Q)
        return pl.ds((n - 1) * PIECE, PIECE)

    def pieces(dirn, t):
        if t < 4:
            return (0, 1, 2, 3, 4)
        return (0, 1, 2) if dirn == 0 else (0, 3, 4)

    rings = {}

    def ring_start(dirn, t, n):
        sgn = 1 - 2 * dirn
        blk = (z - sgn * (t - 1) + 8) % 8
        rows = piece(n, t == 4, dirn)
        src = pf.at[rows] if t == 1 else pa.at[blk, rows]
        rings[dirn, t, n] = start(
            rcopy(src, pa.at[blk, rows], rss.at[dirn, t - 1, n], rrs.at[dirn, t - 1, n], zdev(sgn))
        )

    def page_send(b):
        dz = ORDER[b]

        def one(o, c):
            t = ((z + dz + 8) % 8) * 8 + (yc + o) % 8
            rcopy(ps.at[t], W.at[dec, g], pss.at[b], prs.at[b], (pre, t, rep)).start()
            return c

        lax.fori_loop(1 if dz == 0 else 0, 8, one, 0)

    def batch(b, first=0, count=8):
        return pl.ds(((z - ORDER[b] + 8) % 8) * 8 + first, count)

    def page_wait(b):
        w = W.at[pl.ds(0, 7 if ORDER[b] == 0 else 8), 0]
        c = rcopy(w, w, pss.at[b], prs.at[b], right)
        c.wait_send()
        c.wait_recv()

    xs = {}

    def x_start(b):
        r = W.at[batch(b), g]
        xs[b] = [
            start(rcopy(r, r, xss.at[0, b], xrs.at[0, b], right)),
            start(rcopy(r, r, xss.at[1, b], xrs.at[1, b], left)),
        ]

    def x_forward(b):
        xs[b][0].wait_recv()
        r = W.at[batch(b, 0, 4), g_of(x + 3)]
        xs[b].append(start(rcopy(r, r, xss.at[2, b], xrs.at[2, b], right)))
        xs[b][1].wait_recv()
        r = W.at[batch(b, 4, 4), g_of(x + 1)]
        xs[b].append(start(rcopy(r, r, xss.at[3, b], xrs.at[3, b], left)))

    def x_end(b):
        xs[b][2].wait_recv()
        xs[b][3].wait_recv()

    ys = {}

    def y_start(blk, n):
        r = pa.at[blk, pl.ds(D + g * Q, Q)]
        ys[n] = [
            blk,
            start(rcopy(r, r, yss.at[0, n], yrs.at[0, n], right)),
            start(rcopy(r, r, yss.at[1, n], yrs.at[1, n], left)),
        ]

    def y_forward(n):
        blk = ys[n][0]
        ys[n][1].wait_recv()
        r = pa.at[blk, pl.ds(D + g_of(x + 3) * Q, Q // 2)]
        ys[n].append(start(rcopy(r, r, yss.at[2, n], yrs.at[2, n], right)))
        ys[n][2].wait_recv()
        r = pa.at[blk, pl.ds(D + g_of(x + 1) * Q + Q // 2, Q // 2)]
        ys[n].append(start(rcopy(r, r, yss.at[3, n], yrs.at[3, n], left)))

    def y_end(n):
        ys[n][3].wait_recv()
        ys[n][4].wait_recv()

    def keep(to_lat, to_lse, at, o, l):
        for f in range(4):
            to_lat[f, at, :] = o[:, f * 128 : f * 128 + 128]
        to_lse[at, :] = jnp.broadcast_to(l, (l.shape[0], 128))

    def attend(blk):
        def half(i, c):
            queried = qr[blk, pl.ds(i * 4, 4)].reshape(256, DQ)
            head = queried[:, :DL]
            tail = pa[blk, :, 2 * DL :]
            s0 = nt(head, pa[blk, :, :DL]) + nt(pad_rotary(queried, 0), tail)
            s1 = nt(head, pa[blk, :, DL : 2 * DL]) + nt(pad_rotary(queried, 1), tail)
            top = jnp.maximum(jnp.max(s0, axis=1, keepdims=True), jnp.max(s1, axis=1, keepdims=True))
            w0 = jnp.exp((s0 - top) * SCALE).astype(BF)
            w1 = jnp.exp((s1 - top) * SCALE).astype(BF)
            total = jnp.sum(w0.astype(F32), axis=1, keepdims=True) + jnp.sum(w1.astype(F32), axis=1, keepdims=True)
            o = (nn(w0, pa[blk, :, :DL]) + nn(w1, pa[blk, :, DL : 2 * DL])) / total
            l = top * SCALE + jnp.log(total)
            for n in range(4):
                at = pl.ds(pl.multiple_of((i * 4 + n) * 512 + blk * 64, 64), 64)
                part = slice(n * 64, n * 64 + 64)
                keep(lat, lse, at, o[part], l[part])
            return c

        lax.fori_loop(0, 2, half, 0)

    def masked(s, w_keys, span, lens):
        count = len(lens)
        rows, cols = count * 32, count * span
        r = lax.broadcasted_iota(jnp.int32, (rows, 1), 0) // 32
        limit = jnp.zeros((rows, 1), jnp.int32)
        for n in range(count):
            limit = jnp.where(r == n, lens[n], limit)
        c = lax.broadcasted_iota(jnp.int32, (rows, cols), 1) - r * span
        ok = (c >= 0) & (c < limit)
        s = jnp.where(ok, s * SCALE, NEG)
        m = jnp.max(s, axis=1, keepdims=True)
        w = jnp.where(ok, jnp.exp(s - m), 0.0).astype(BF)
        l = jnp.sum(w.astype(F32), axis=1, keepdims=True)
        l = jnp.where(l > 0.0, l, 1.0)
        return nn(w, w_keys) / l, m + jnp.log(l)

    def resident(i):
        queried = q[pl.ds(i * 8, 8)].reshape(256, DQ)
        keys = suffix[pl.ds(i * 8, 8)].reshape(256, DQ)
        o, l = masked(nt(queried, keys), keys[:, :DL], 32, [slen[i * 8 + n] for n in range(8)])
        keep(latr, lser, pl.ds(pl.multiple_of(i * 256, 256), 256), o, l)

    def residents(i, j):
        def one(n, c):
            resident(n)
            return c

        lax.fori_loop(i, j, one, 0)

    def page_attend(b):
        base = ((z - ORDER[b] + 8) % 8) * 8

        def one(i, c):
            src = base + i * 4
            tail = W[pl.ds(src, 4), :, :, 2 * DL :].reshape(256, 128)
            for k in range(2):
                slots = [(src + n) * 2 + k for n in range(4)]
                queried = jnp.concatenate([q[req[v]] for v in slots], axis=0)
                keys = W[pl.ds(src, 4), :, :, k * DL : k * DL + DL].reshape(256, DL)
                s = nt(queried[:, :DL], keys) + nt(pad_rotary(queried, k), tail)
                o, l = masked(s, keys, 64, [length[v] for v in slots])
                for n in range(4):
                    part = slice(n * 32, n * 32 + 32)
                    keep(lat, lse, pl.ds(pl.multiple_of(slots[n] * 32, 32), 32), o[part], l[part])
            return c

        lax.fori_loop(0, 2, one, 0)

    def gathered(ref, rows):
        return jnp.concatenate([ref[f, rows, :] for f in range(4)], axis=1).astype(BF)

    lane = lax.broadcasted_iota(jnp.int32, (128, 128), 1)

    for n in range(5):
        ring_start(0, 1, n)
        ring_start(1, 1, n)
        if n == 0:
            for b in PLAN[0]:
                page_send(b)
        else:
            for m in range(7):
                query_send(n - 1, m)
    loads[0].wait()
    loads[1].wait()
    for t in range(1, 5):
        if t < 3:
            residents(4 * t - 4, 4 * t)
        if t == 3:
            own_q.wait()
            own_p.wait()
            for n in range(7):
                query_wait(n).wait_recv()
            attend(z)
            y_end(0)
            y_end(1)
            attend((z + 7) % 8)
            attend((z + 1) % 8)
            y_end(2)
            y_end(3)
            attend((z + 6) % 8)
            attend((z + 2) % 8)
        for n in range(5):
            for dirn in (0, 1):
                if n not in pieces(dirn, t):
                    continue
                rings[dirn, t, n].wait_recv()
                if t < 4 and n in pieces(dirn, t + 1):
                    ring_start(dirn, t + 1, n)
                if n == 0 and t < 4:
                    y_start((z - t + 8) % 8 if dirn == 0 else (z + t) % 8, 2 * t - 2 + dirn)
            if t == 4 and n == 0:
                y_start((z + 4) % 8, 6)
        if t < 4:
            for b in PLAN[t]:
                page_send(b)
        if t == 1:
            own_w.wait()
        for b in PLAN[t - 1]:
            page_wait(b)
            x_start(b)
        if t == 4:
            y_forward(6)
        else:
            y_forward(2 * t - 2)
            y_forward(2 * t - 1)
        if t < 4:
            for b in PLAN[t - 1]:
                x_forward(b)
    y_end(4)
    y_end(5)
    attend((z + 5) % 8)
    attend((z + 3) % 8)
    for b in PLAN[3]:
        x_forward(b)
    y_end(6)
    attend((z + 4) % 8)
    loads[2].wait()

    def project(h, c):
        rows = pl.ds(h, 128, stride=32)
        outs[h] = nn(gathered(lat, rows), vu[h]).astype(BF)
        return jnp.where(lane == h, lse[rows, :], c)

    lses[...] = lax.fori_loop(0, 32, project, jnp.zeros((128, 128), F32), unroll=2)

    back = []
    for n in range(7):
        dy, dc = DQDS[n]
        t = peer(dy, dc)
        there, here = pl.ds(t * 16, 16), pl.ds(yc * 16, 16)
        dev = (pre, z * 8 + t, rep)
        back.append(start(rcopy(outs.at[:, there], ret.at[:, here], bss.at[0, n], brs.at[0, n], dev)))
        back.append(start(rcopy(lses.at[there], rlse.at[here], bss.at[1, n], brs.at[1, n], dev)))
    here = pl.ds(yc * 16, 16)
    mine = [
        start(pltpu.make_async_copy(outs.at[:, here], ret.at[:, here], loc.at[3])),
        start(pltpu.make_async_copy(lses.at[here], rlse.at[here], loc.at[4])),
    ]

    for b in range(8):
        x_end(b)
        page_attend(b)

    for c in back:
        c.wait()
    for c in mine:
        c.wait()

    def column(h, c):
        return jnp.where(lane == h, lse[pl.ds(h, 128, stride=32), :], c)

    lses[...] = jnp.transpose(lax.fori_loop(0, 32, column, jnp.zeros((128, 128), F32), unroll=8))
    hot = lax.broadcasted_iota(jnp.int32, (64, 128), 1) == slot[...]
    pick = hot.astype(BF)
    mem = lax.broadcasted_iota(jnp.int32, (64, 128), 0) == member[...]
    plse = jnp.dot(hot.astype(F32), rlse[...], precision=lax.Precision.HIGHEST, preferred_element_type=F32)

    def finish(h, c):
        rows = pl.ds(h, 64, stride=32)
        lp = jnp.sum(jnp.where(lane[:64] == h, plse, 0.0), axis=1, keepdims=True)
        lr = lser[rows, :][:, :1]
        lw = jnp.where(mem, lses[pl.ds(h, 1), :], NEG)
        high = jnp.maximum(jnp.maximum(lp, lr), jnp.max(lw, axis=1, keepdims=True))
        wp, wr = jnp.exp(lp - high), jnp.exp(lr - high)
        ww = jnp.where(mem, jnp.exp(lw - high), 0.0).astype(BF)
        below = wp + wr + jnp.sum(ww.astype(F32), axis=1, keepdims=True)
        v = vu[h]
        paged = nn(ww, nn(gathered(lat, pl.ds(h, 128, stride=32)), v).astype(BF))
        total = wp * nn(pick, ret[h]) + wr * nn(gathered(latr, rows), v) + paged
        out[:, pl.ds(pl.multiple_of(h * 128, 128), 128)] = (total / below).astype(BF)
        return c

    lax.fori_loop(0, 32, finish, 0, unroll=4)

    for n in range(7):
        query_wait(n).wait_send()
        for c in ys[n][1:]:
            c.wait_send()
    for c in rings.values():
        c.wait_send()
    for b in range(8):
        for c in xs[b]:
            c.wait_send()


def exchange(req, length, slen, qs, pf, ps, q, suffix, vu, slot, member):
    S = pltpu.SemaphoreType.DMA
    return pl.pallas_call(
        exchange_kernel,
        out_shape=jax.ShapeDtypeStruct((64, 4096), BF),
        in_specs=[SM, SM, SM] + [ANY] * 6 + [VM, VM],
        out_specs=VM,
        scratch_shapes=[
            pltpu.VMEM((64, 4, 16, DP), BF),
            pltpu.VMEM((8, 8, 2, 32, DQ), BF),
            pltpu.VMEM((8, 512, DP), BF),
            pltpu.VMEM((4, 4096, 128), F32),
            pltpu.VMEM((4096, 128), F32),
            pltpu.VMEM((4, 2048, 128), F32),
            pltpu.VMEM((2048, 128), F32),
            pltpu.VMEM((32, 128, 128), BF),
            pltpu.VMEM((128, 128), F32),
            pltpu.VMEM((32, 128, 128), BF),
            pltpu.VMEM((128, 128), F32),
            pltpu.VMEM((64, 32, DQ), BF),
            pltpu.VMEM((64, 32, DQ), BF),
            pltpu.VMEM((32, DL, 128), BF),
            S((7,)), S((7,)), S((2, 4, 5)), S((2, 4, 5)), S((8,)), S((8,)),
            S((4, 8)), S((4, 8)), S((4, 7)), S((4, 7)), S((2, 7)), S((2, 7)), S((8,)),
        ],
        compiler_params=pltpu.CompilerParams(
            collective_id=0, has_side_effects=True, vmem_limit_bytes=60 * 2**20
        ),
    )(req, length, slen, qs, pf, ps, q, suffix, vu, slot, member)


def per_device(
    queries, prefix_of, prefix_cache, suffix_cache, suffix_len, fresh_pages,
    page_owner, page_request, page_tokens, value_up,
):
    dec = lax.axis_index("dec")
    qs, ps, pp, slot = bucket(prefix_of[:, 0], page_owner[:, 0], queries, fresh_pages, prefix_cache[0])

    mine = page_owner[:, 0].reshape(64, 64) == dec
    nth = jnp.cumsum(mine.astype(jnp.int32), axis=1)
    pick = mine[:, None, :] & (nth[:, None, :] == jnp.arange(1, 3)[None, :, None])
    req = jnp.sum(jnp.where(pick, page_request.reshape(64, 1, 64), 0), axis=2).reshape(128)
    length = jnp.sum(jnp.where(pick, page_tokens.reshape(64, 1, 64), 0), axis=2).reshape(128)
    member = jnp.where(length > 0, req, -1).reshape(1, 128)
    return exchange(
        req, length, suffix_len, qs, pp, ps, queries, suffix_cache, value_up,
        slot.reshape(64, 1), member,
    )


def solution(mesh):
    heads = ("pre", "rep")
    placed = (
        P("dec", heads, None),
        P("dec", None),
        P("dec", None, None),
        P("dec", None, None),
        P("dec"),
        P("dec", heads, None),
        P(),
        P(),
        P(),
        P(heads, None, None),
    )
    return jax.shard_map(
        per_device, mesh=mesh, in_specs=placed, out_specs=P("dec", heads), check_vma=False
    )
```

```python
import functools

import jax
import jax.numpy as jnp
from jax import lax
from jax.experimental import pallas as pl
from jax.experimental.pallas import tpu as pltpu
from jax.sharding import PartitionSpec as P

MESH = pl.DeviceIdType.MESH
BF, F32 = jnp.bfloat16, jnp.float32
ANY = pl.BlockSpec(memory_space=pl.ANY)
VM = pl.BlockSpec(memory_space=pltpu.VMEM)
SM = pl.BlockSpec(memory_space=pltpu.SMEM)
DL, DQ = 512, 576
DP = 1152
SCALE = 192.0**-0.5
NEG = -1e30
ORDER = (0, 1, -1, 2, -2, 3, -3, 4)
PLAN = ((0, 1, 2), (3, 4), (5, 6), (7,))
D, Q = 256, 64
PIECE = 64
DQDS = (((1, 0)), ((-1, 0)), ((1, 1)), ((-1, 1)), ((2, 0)), ((2, 1)), ((0, 1)))


def bucket_kernel(
    pref, owner, q_hbm, f_hbm, p_hbm, qs_hbm, ps_hbm, pp_hbm, slot, count, queries, fresh, prefix, qs, ps, pp, sem
):
    dec = lax.axis_index("dec")
    loads = [
        pltpu.make_async_copy(p_hbm, prefix, sem.at[0]),
        pltpu.make_async_copy(f_hbm, fresh, sem.at[1]),
        pltpu.make_async_copy(q_hbm, queries, sem.at[2]),
    ]
    stores = [
        pltpu.make_async_copy(pp, pp_hbm, sem.at[3]),
        pltpu.make_async_copy(ps, ps_hbm, sem.at[4]),
        pltpu.make_async_copy(qs, qs_hbm, sem.at[5]),
    ]
    for c in loads:
        c.start()
    qs[...] = jnp.zeros_like(qs)
    ps[...] = jnp.zeros_like(ps)

    def clear(i, c):
        count[0, i] = 0
        count[1, i] = 0
        return c

    lax.fori_loop(0, 64, clear, 0, unroll=8)
    half = lax.broadcasted_iota(jnp.int32, (16, 128), 1) // 64
    loads[0].wait()
    pp[:, :DL] = prefix[:512, :DL]
    pp[:, DL : 2 * DL] = prefix[512:, :DL]
    pp[:, 2 * DL :] = jnp.concatenate([prefix[:512, DL:], prefix[512:, DL:]], axis=1)
    stores[0].start()

    def put_page(i, c):
        o = owner[dec * 64 + i]
        k = count[1, o]
        count[1, o] = k + 1
        page = fresh[i]
        ps[o, :, pl.ds(pl.multiple_of(k * DL, DL), DL)] = page[:, :DL]
        rotary = page[:, DL:].astype(F32)
        both = jnp.concatenate([rotary, rotary], axis=1)
        ps[o, :, 2 * DL :] = jnp.where(half == k, both, ps[o, :, 2 * DL :].astype(F32)).astype(BF)
        return c

    def put_query(i, c):
        p = pref[i]
        k = count[0, p]
        count[0, p] = k + 1
        to = (p % 8) * 16 + (p // 8) * 2 + k
        qs[to] = queries[i]
        slot[i] = to
        return c

    loads[1].wait()
    lax.fori_loop(0, 64, put_page, 0)
    stores[1].start()
    loads[2].wait()
    lax.fori_loop(0, 64, put_query, 0)
    stores[2].start()
    for c in stores:
        c.wait()


def bucket(pref, owner, queries, fresh, prefix):
    qs, ps, pp, slot = pl.pallas_call(
        bucket_kernel,
        out_shape=(
            jax.ShapeDtypeStruct((128, 32, DQ), BF),
            jax.ShapeDtypeStruct((64, 16, DP), BF),
            jax.ShapeDtypeStruct((512, DP), BF),
            jax.ShapeDtypeStruct((64,), jnp.int32),
        ),
        in_specs=[SM, SM, ANY, ANY, ANY],
        out_specs=(ANY, ANY, ANY, SM),
        scratch_shapes=[
            pltpu.SMEM((2, 64), jnp.int32),
            pltpu.VMEM((64, 32, DQ), BF),
            pltpu.VMEM((64, 16, DQ), BF),
            pltpu.VMEM((1024, DQ), BF),
            pltpu.VMEM((128, 32, DQ), BF),
            pltpu.VMEM((64, 16, DP), BF),
            pltpu.VMEM((512, DP), BF),
            pltpu.SemaphoreType.DMA((6,)),
        ],
        compiler_params=pltpu.CompilerParams(vmem_limit_bytes=60 * 2**20),
    )(pref, owner, queries, fresh, prefix)
    return qs.reshape(8, 8, 2, 32, DQ), ps, pp, slot


def rcopy(src, dst, ss, rs, dev):
    return pltpu.make_async_remote_copy(
        src_ref=src, dst_ref=dst, send_sem=ss, recv_sem=rs, device_id=dev, device_id_type=MESH
    )


def nt(a, b):
    return lax.dot_general(a, b, (((1,), (1,)), ((), ())), preferred_element_type=F32)


def nn(a, b):
    return jnp.dot(a, b, preferred_element_type=F32)


def pad_rotary(q, k):
    r = q[:, DL:]
    zero = jnp.zeros_like(r)
    return jnp.concatenate([zero, r] if k else [r, zero], axis=1)


def exchange_kernel(
    req, length, slen, qs, pf, ps, q_hbm, suffix_hbm, vu_hbm, slot, member, out,
    W, qr, pa, lat, lse, latr, lser, outs, lses, ret, rlse, q, suffix, vu,
    qss, qrs, rss, rrs, pss, prs, xss, xrs, yss, yrs, bss, brs, loc,
):
    pre, dec, rep = lax.axis_index("pre"), lax.axis_index("dec"), lax.axis_index("rep")
    z, y, core = dec // 8, (dec // 2) % 4, dec % 2
    yc = dec % 8
    x = rep * 2 + pre
    g = pre * 2 + rep

    def at_x(v):
        v = v % 4
        return (v % 2, dec, v // 2)

    def g_of(v):
        v = v % 4
        return (v % 2) * 2 + v // 2

    right, left = at_x(x + 1), at_x(x + 3)
    bar = pltpu.get_barrier_semaphore()

    def hello(o, c):
        pl.semaphore_signal(bar, inc=1, device_id=(pre, (dec + o) % 64, rep), device_id_type=MESH)
        return c

    lax.fori_loop(1, 64, hello, 0)
    pl.semaphore_signal(bar, inc=1, device_id=right, device_id_type=MESH)
    pl.semaphore_signal(bar, inc=1, device_id=left, device_id_type=MESH)
    pl.semaphore_wait(bar, 65)

    def start(c):
        c.start()
        return c

    own_q = start(pltpu.make_async_copy(qs.at[yc], qr.at[:, yc], loc.at[0]))
    own_p = start(pltpu.make_async_copy(pf, pa.at[z], loc.at[1]))
    own_w = start(pltpu.make_async_copy(ps.at[dec], W.at[dec, g], loc.at[2]))
    loads = [
        start(pltpu.make_async_copy(q_hbm, q, loc.at[5])),
        start(pltpu.make_async_copy(suffix_hbm, suffix, loc.at[6])),
        start(pltpu.make_async_copy(vu_hbm, vu, loc.at[7])),
    ]

    def peer(dy, dc):
        return ((y + dy + 4) % 4) * 2 + (core + dc) % 2

    def query_send(j, n):
        dy, dc = DQDS[n]
        t = peer(dy, dc)
        part = pl.ds(2 * j, 2)
        return start(rcopy(qs.at[t, part], qr.at[part, yc], qss.at[n], qrs.at[n], (pre, z * 8 + t, rep)))

    def query_wait(n):
        dy, dc = DQDS[n]
        s = peer(-dy, dc)
        return rcopy(qs.at[0], qr.at[:, s], qss.at[n], qrs.at[n], (pre, z * 8 + s, rep))

    def zdev(dz):
        return (pre, ((z + dz + 8) % 8) * 8 + yc, rep)

    def piece(n, last, dirn):
        if n == 0:
            return pl.ds(D + g * Q + dirn * (Q // 2), Q // 2) if last else pl.ds(D + g * Q, Q)
        return pl.ds((n - 1) * PIECE, PIECE)

    def pieces(dirn, t):
        if t < 4:
            return (0, 1, 2, 3, 4)
        return (0, 1, 2) if dirn == 0 else (0, 3, 4)

    rings = {}

    def ring_start(dirn, t, n):
        sgn = 1 - 2 * dirn
        blk = (z - sgn * (t - 1) + 8) % 8
        rows = piece(n, t == 4, dirn)
        src = pf.at[rows] if t == 1 else pa.at[blk, rows]
        rings[dirn, t, n] = start(
            rcopy(src, pa.at[blk, rows], rss.at[dirn, t - 1, n], rrs.at[dirn, t - 1, n], zdev(sgn))
        )

    def page_send(b):
        dz = ORDER[b]

        def one(o, c):
            t = ((z + dz + 8) % 8) * 8 + (yc + o) % 8
            rcopy(ps.at[t], W.at[dec, g], pss.at[b], prs.at[b], (pre, t, rep)).start()
            return c

        lax.fori_loop(1 if dz == 0 else 0, 8, one, 0)

    def batch(b, first=0, count=8):
        return pl.ds(((z - ORDER[b] + 8) % 8) * 8 + first, count)

    def page_wait(b):
        w = W.at[pl.ds(0, 7 if ORDER[b] == 0 else 8), 0]
        c = rcopy(w, w, pss.at[b], prs.at[b], right)
        c.wait_send()
        c.wait_recv()

    xs = {}

    def x_start(b):
        r = W.at[batch(b), g]
        xs[b] = [
            start(rcopy(r, r, xss.at[0, b], xrs.at[0, b], right)),
            start(rcopy(r, r, xss.at[1, b], xrs.at[1, b], left)),
        ]

    def x_forward(b):
        xs[b][0].wait_recv()
        r = W.at[batch(b, 0, 4), g_of(x + 3)]
        xs[b].append(start(rcopy(r, r, xss.at[2, b], xrs.at[2, b], right)))
        xs[b][1].wait_recv()
        r = W.at[batch(b, 4, 4), g_of(x + 1)]
        xs[b].append(start(rcopy(r, r, xss.at[3, b], xrs.at[3, b], left)))

    def x_end(b):
        xs[b][2].wait_recv()
        xs[b][3].wait_recv()

    ys = {}

    def y_start(blk, n):
        r = pa.at[blk, pl.ds(D + g * Q, Q)]
        ys[n] = [
            blk,
            start(rcopy(r, r, yss.at[0, n], yrs.at[0, n], right)),
            start(rcopy(r, r, yss.at[1, n], yrs.at[1, n], left)),
        ]

    def y_forward(n):
        blk = ys[n][0]
        ys[n][1].wait_recv()
        r = pa.at[blk, pl.ds(D + g_of(x + 3) * Q, Q // 2)]
        ys[n].append(start(rcopy(r, r, yss.at[2, n], yrs.at[2, n], right)))
        ys[n][2].wait_recv()
        r = pa.at[blk, pl.ds(D + g_of(x + 1) * Q + Q // 2, Q // 2)]
        ys[n].append(start(rcopy(r, r, yss.at[3, n], yrs.at[3, n], left)))

    def y_end(n):
        ys[n][3].wait_recv()
        ys[n][4].wait_recv()

    def keep(to_lat, to_lse, at, o, l):
        for f in range(4):
            to_lat[f, at, :] = o[:, f * 128 : f * 128 + 128]
        to_lse[at, :] = jnp.broadcast_to(l, (l.shape[0], 128))

    def attend(blk):
        def half(i, c):
            queried = qr[blk, pl.ds(i * 4, 4)].reshape(256, DQ)
            head = queried[:, :DL]
            tail = pa[blk, :, 2 * DL :]
            s0 = nt(head, pa[blk, :, :DL]) + nt(pad_rotary(queried, 0), tail)
            s1 = nt(head, pa[blk, :, DL : 2 * DL]) + nt(pad_rotary(queried, 1), tail)
            top = jnp.maximum(jnp.max(s0, axis=1, keepdims=True), jnp.max(s1, axis=1, keepdims=True))
            w0 = jnp.exp((s0 - top) * SCALE).astype(BF)
            w1 = jnp.exp((s1 - top) * SCALE).astype(BF)
            total = jnp.sum(w0.astype(F32), axis=1, keepdims=True) + jnp.sum(w1.astype(F32), axis=1, keepdims=True)
            o = (nn(w0, pa[blk, :, :DL]) + nn(w1, pa[blk, :, DL : 2 * DL])) / total
            l = top * SCALE + jnp.log(total)
            for n in range(4):
                at = pl.ds(pl.multiple_of((i * 4 + n) * 512 + blk * 64, 64), 64)
                part = slice(n * 64, n * 64 + 64)
                keep(lat, lse, at, o[part], l[part])
            return c

        lax.fori_loop(0, 2, half, 0)

    def masked(s, w_keys, span, lens):
        count = len(lens)
        rows, cols = count * 32, count * span
        r = lax.broadcasted_iota(jnp.int32, (rows, 1), 0) // 32
        limit = jnp.zeros((rows, 1), jnp.int32)
        for n in range(count):
            limit = jnp.where(r == n, lens[n], limit)
        c = lax.broadcasted_iota(jnp.int32, (rows, cols), 1) - r * span
        ok = (c >= 0) & (c < limit)
        s = jnp.where(ok, s * SCALE, NEG)
        m = jnp.max(s, axis=1, keepdims=True)
        w = jnp.where(ok, jnp.exp(s - m), 0.0).astype(BF)
        l = jnp.sum(w.astype(F32), axis=1, keepdims=True)
        l = jnp.where(l > 0.0, l, 1.0)
        return nn(w, w_keys) / l, m + jnp.log(l)

    def resident(i):
        queried = q[pl.ds(i * 8, 8)].reshape(256, DQ)
        keys = suffix[pl.ds(i * 8, 8)].reshape(256, DQ)
        o, l = masked(nt(queried, keys), keys[:, :DL], 32, [slen[i * 8 + n] for n in range(8)])
        keep(latr, lser, pl.ds(pl.multiple_of(i * 256, 256), 256), o, l)

    def residents(i, j):
        def one(n, c):
            resident(n)
            return c

        lax.fori_loop(i, j, one, 0)

    def page_attend(b):
        base = ((z - ORDER[b] + 8) % 8) * 8

        def one(i, c):
            src = base + i * 4
            tail = W[pl.ds(src, 4), :, :, 2 * DL :].reshape(256, 128)
            for k in range(2):
                slots = [(src + n) * 2 + k for n in range(4)]
                queried = jnp.concatenate([q[req[v]] for v in slots], axis=0)
                keys = W[pl.ds(src, 4), :, :, k * DL : k * DL + DL].reshape(256, DL)
                s = nt(queried[:, :DL], keys) + nt(pad_rotary(queried, k), tail)
                o, l = masked(s, keys, 64, [length[v] for v in slots])
                for n in range(4):
                    part = slice(n * 32, n * 32 + 32)
                    keep(lat, lse, pl.ds(pl.multiple_of(slots[n] * 32, 32), 32), o[part], l[part])
            return c

        lax.fori_loop(0, 2, one, 0)

    def gathered(ref, rows):
        return jnp.concatenate([ref[f, rows, :] for f in range(4)], axis=1).astype(BF)

    lane = lax.broadcasted_iota(jnp.int32, (128, 128), 1)

    for n in range(5):
        ring_start(0, 1, n)
        ring_start(1, 1, n)
        if n == 0:
            for b in PLAN[0]:
                page_send(b)
        else:
            for m in range(7):
                query_send(n - 1, m)
    loads[0].wait()
    loads[1].wait()
    for t in range(1, 5):
        if t < 3:
            residents(4 * t - 4, 4 * t)
        if t == 3:
            own_q.wait()
            own_p.wait()
            for n in range(7):
                query_wait(n).wait_recv()
            attend(z)
            y_end(0)
            y_end(1)
            attend((z + 7) % 8)
            attend((z + 1) % 8)
            y_end(2)
            y_end(3)
            attend((z + 6) % 8)
            attend((z + 2) % 8)
        for n in range(5):
            for dirn in (0, 1):
                if n not in pieces(dirn, t):
                    continue
                rings[dirn, t, n].wait_recv()
                if t < 4 and n in pieces(dirn, t + 1):
                    ring_start(dirn, t + 1, n)
                if n == 0 and t < 4:
                    y_start((z - t + 8) % 8 if dirn == 0 else (z + t) % 8, 2 * t - 2 + dirn)
            if t == 4 and n == 0:
                y_start((z + 4) % 8, 6)
        if t < 4:
            for b in PLAN[t]:
                page_send(b)
        if t == 1:
            own_w.wait()
        for b in PLAN[t - 1]:
            page_wait(b)
            x_start(b)
        if t == 4:
            y_forward(6)
        else:
            y_forward(2 * t - 2)
            y_forward(2 * t - 1)
        if t < 4:
            for b in PLAN[t - 1]:
                x_forward(b)
    y_end(4)
    attend((z + 5) % 8)
    for b in PLAN[3]:
        x_forward(b)
    y_end(5)
    attend((z + 3) % 8)
    y_end(6)
    attend((z + 4) % 8)
    loads[2].wait()

    def project(h, c):
        rows = pl.ds(h, 128, stride=32)
        outs[h] = nn(gathered(lat, rows), vu[h]).astype(BF)
        return jnp.where(lane == h, lse[rows, :], c)

    lses[...] = lax.fori_loop(0, 32, project, jnp.zeros((128, 128), F32), unroll=2)

    back = []
    for n in range(7):
        dy, dc = DQDS[n]
        t = peer(dy, dc)
        there, here = pl.ds(t * 16, 16), pl.ds(yc * 16, 16)
        dev = (pre, z * 8 + t, rep)
        back.append(start(rcopy(outs.at[:, there], ret.at[:, here], bss.at[0, n], brs.at[0, n], dev)))
        back.append(start(rcopy(lses.at[there], rlse.at[here], bss.at[1, n], brs.at[1, n], dev)))
    here = pl.ds(yc * 16, 16)
    mine = [
        start(pltpu.make_async_copy(outs.at[:, here], ret.at[:, here], loc.at[3])),
        start(pltpu.make_async_copy(lses.at[here], rlse.at[here], loc.at[4])),
    ]

    for b in range(8):
        x_end(b)
        page_attend(b)

    for c in back:
        c.wait()
    for c in mine:
        c.wait()

    def column(h, c):
        return jnp.where(lane == h, lse[pl.ds(h, 128, stride=32), :], c)

    lses[...] = jnp.transpose(lax.fori_loop(0, 32, column, jnp.zeros((128, 128), F32), unroll=8))
    hot = lax.broadcasted_iota(jnp.int32, (64, 128), 1) == slot[...]
    pick = hot.astype(BF)
    mem = lax.broadcasted_iota(jnp.int32, (64, 128), 0) == member[...]
    plse = jnp.dot(hot.astype(F32), rlse[...], precision=lax.Precision.HIGHEST, preferred_element_type=F32)

    def finish(h, c):
        rows = pl.ds(h, 64, stride=32)
        lp = jnp.sum(jnp.where(lane[:64] == h, plse, 0.0), axis=1, keepdims=True)
        lr = lser[rows, :][:, :1]
        lw = jnp.where(mem, lses[pl.ds(h, 1), :], NEG)
        high = jnp.maximum(jnp.maximum(lp, lr), jnp.max(lw, axis=1, keepdims=True))
        wp, wr = jnp.exp(lp - high), jnp.exp(lr - high)
        ww = jnp.where(mem, jnp.exp(lw - high), 0.0).astype(BF)
        below = wp + wr + jnp.sum(ww.astype(F32), axis=1, keepdims=True)
        v = vu[h]
        paged = nn(ww, nn(gathered(lat, pl.ds(h, 128, stride=32)), v).astype(BF))
        total = wp * nn(pick, ret[h]) + wr * nn(gathered(latr, rows), v) + paged
        out[:, pl.ds(pl.multiple_of(h * 128, 128), 128)] = (total / below).astype(BF)
        return c

    lax.fori_loop(0, 32, finish, 0, unroll=4)

    for n in range(7):
        query_wait(n).wait_send()
        for c in ys[n][1:]:
            c.wait_send()
    for c in rings.values():
        c.wait_send()
    for b in range(8):
        for c in xs[b]:
            c.wait_send()


def exchange(req, length, slen, qs, pf, ps, q, suffix, vu, slot, member):
    S = pltpu.SemaphoreType.DMA
    return pl.pallas_call(
        exchange_kernel,
        out_shape=jax.ShapeDtypeStruct((64, 4096), BF),
        in_specs=[SM, SM, SM] + [ANY] * 6 + [VM, VM],
        out_specs=VM,
        scratch_shapes=[
            pltpu.VMEM((64, 4, 16, DP), BF),
            pltpu.VMEM((8, 8, 2, 32, DQ), BF),
            pltpu.VMEM((8, 512, DP), BF),
            pltpu.VMEM((4, 4096, 128), F32),
            pltpu.VMEM((4096, 128), F32),
            pltpu.VMEM((4, 2048, 128), F32),
            pltpu.VMEM((2048, 128), F32),
            pltpu.VMEM((32, 128, 128), BF),
            pltpu.VMEM((128, 128), F32),
            pltpu.VMEM((32, 128, 128), BF),
            pltpu.VMEM((128, 128), F32),
            pltpu.VMEM((64, 32, DQ), BF),
            pltpu.VMEM((64, 32, DQ), BF),
            pltpu.VMEM((32, DL, 128), BF),
            S((7,)), S((7,)), S((2, 4, 5)), S((2, 4, 5)), S((8,)), S((8,)),
            S((4, 8)), S((4, 8)), S((4, 7)), S((4, 7)), S((2, 7)), S((2, 7)), S((8,)),
        ],
        compiler_params=pltpu.CompilerParams(
            collective_id=0, has_side_effects=True, vmem_limit_bytes=60 * 2**20
        ),
    )(req, length, slen, qs, pf, ps, q, suffix, vu, slot, member)


def per_device(
    queries, prefix_of, prefix_cache, suffix_cache, suffix_len, fresh_pages,
    page_owner, page_request, page_tokens, value_up,
):
    dec = lax.axis_index("dec")
    qs, ps, pp, slot = bucket(prefix_of[:, 0], page_owner[:, 0], queries, fresh_pages, prefix_cache[0])

    mine = page_owner[:, 0].reshape(64, 64) == dec
    nth = jnp.cumsum(mine.astype(jnp.int32), axis=1)
    pick = mine[:, None, :] & (nth[:, None, :] == jnp.arange(1, 3)[None, :, None])
    req = jnp.sum(jnp.where(pick, page_request.reshape(64, 1, 64), 0), axis=2).reshape(128)
    length = jnp.sum(jnp.where(pick, page_tokens.reshape(64, 1, 64), 0), axis=2).reshape(128)
    member = jnp.where(length > 0, req, -1).reshape(1, 128)
    return exchange(
        req, length, suffix_len, qs, pp, ps, queries, suffix_cache, value_up,
        slot.reshape(64, 1), member,
    )


def solution(mesh):
    heads = ("pre", "rep")
    placed = (
        P("dec", heads, None),
        P("dec", None),
        P("dec", None, None),
        P("dec", None, None),
        P("dec"),
        P("dec", heads, None),
        P(),
        P(),
        P(),
        P(heads, None, None),
    )
    return jax.shard_map(
        per_device, mesh=mesh, in_specs=placed, out_specs=P("dec", heads), check_vma=False
    )
```
